128 devices in a mesh: row: 4 (over z), col: 32 (over x, y, core).
Axes of the slice: x: 4, y: 4, z: 4, core: 2. Of those that a mesh axis runs over, the one named last changes fastest.
Arguments:
- embeddings: bfloat16 [65536, 256], P(('row', 'col')), may hold values from -6 to 6
- partition_source: int32 [65536], P(('row', 'col')), may hold values from 0 to 65535, as said below
- hash_target: int32 [65536], P(('row', 'col')), may hold values from 0 to 65535, as said below
- tile_values: bfloat16 [12288, 128, 128], P(('row', 'col')), may hold values from -0.109375 to 0.109375
- tile_row: int32 [12288], P(('row', 'col')), may hold values from 0 to 3
- tile_owner: int32 [12288, 1], P(('row', 'col')), may hold values from 0 to 31; in each aligned block of 96 rows (0 to 95, 96 to 191, ...) at most 4 rows name the same one
- tile_sub: int32 [12288], P(('row', 'col')), may hold values from 0 to 3
- tile_count: int32 [128], P(('row', 'col')), may hold values from 1 to 96, as said below
- cotangent: bfloat16 [65536, 256], P(('row', 'col')), may hold values from -6 to 6
Outputs:
- propagated: bfloat16 [65536, 256], P(('row', 'col'))
- embed_grad: bfloat16 [65536, 256], P(('row', 'col'))
The draws below stay inside these ranges and needn't reach their ends.
Inputs may be any that keep to these rules, and one draw needn't show every extreme that they name: `partition_source`: A permutation of the nodes; for every two devices, exactly 4 of the first device's hash rows are named at the second device's partition rows. `hash_target`: the inverse of partition_source. `tile_count`: some device uses all 96 slots in every draw. `tile_owner`: among the 96 slots of one device no value is named by more than 4 slots.
All inputs are finite; a program needn't handle non-finite values.
Results may differ from the reference program's by a relative error of at most 0.017.
Values may be sent and summed in bfloat16 or wider, within the bound.
No kernel may reach another device: no remote copies, remote signals or barrier semaphores. Data moves between devices by JAX's collectives and lax.ppermute only.
A program may use at most 192 MiB of HBM per device.

```python
import math
import jax
import jax.numpy as jnp
import numpy as np
from jax import lax

WIDTH = 256
TILE = 128
NODES_DEV = 512
SLOTS = 96
ROW_BLOCKS = 4
NODES = 65536
OWNER_CAP = 4
N_ROW = 4
N_COL = 32
DEVICES = 128


def placement_pair(key):
    peer_rows = NODES_DEV // DEVICES
    source_keys = jax.random.split(jax.random.fold_in(key, 1), DEVICES)
    target_keys = jax.random.split(jax.random.fold_in(key, 2), DEVICES)
    source_perm = jax.vmap(lambda inner: jax.random.permutation(inner, NODES_DEV))(source_keys).astype(jnp.int32)
    target_perm = jax.vmap(lambda inner: jax.random.permutation(inner, NODES_DEV))(target_keys).astype(jnp.int32)
    triple = jnp.arange(NODES, dtype=jnp.int32)
    source_dev = triple // NODES_DEV
    within = triple % NODES_DEV
    target_dev = within // peer_rows
    offset = within % peer_rows
    hash_rows = source_dev * NODES_DEV + source_perm[source_dev, within]
    part_rows = target_dev * NODES_DEV + target_perm[target_dev, source_dev * peer_rows + offset]
    forward = jnp.zeros((NODES,), jnp.int32).at[part_rows].set(hash_rows)
    inverse = jnp.zeros((NODES,), jnp.int32).at[hash_rows].set(part_rows)
    return (forward, inverse)


def draw_partition_source(key, part):
    return placement_pair(key)[0]


def draw_hash_target(key, part):
    return placement_pair(key)[1]


def draw_tile_count(key, part):
    key = jax.random.fold_in(key, 7)
    shifts = jax.random.randint(jax.random.fold_in(key, 1), (DEVICES,), 0, 4)
    divisor = jnp.array([1, 2, 4, 8], jnp.int32)[shifts]
    counts = jnp.maximum(SLOTS // divisor, 1).astype(jnp.int32)
    busiest = jax.random.randint(jax.random.fold_in(key, 2), (), 0, DEVICES)
    return counts.at[busiest].set(SLOTS).astype(jnp.int32)


def touch_ends(values, rng, low, top_value):
    extent = values.shape
    place = [jax.random.randint(jax.random.fold_in(rng, axis), (), 0, extent[axis]) for axis in range(len(extent))]
    values = values.at[tuple(place)].set(low)
    longest = extent.index(max(extent))
    place[longest] = (place[longest] + 1) % extent[longest]
    return values.at[tuple(place)].set(top_value)


def block_levels(stream_key, dims, cuts, least, largest):
    def one(dim, parts):
        steps = jax.random.uniform(jax.random.fold_in(jax.random.fold_in(stream_key, 6), dim), (parts,), jnp.float32, least / len(cuts), largest / len(cuts))
        return jnp.repeat(jnp.exp(steps), dims[dim] // parts).reshape((-1,) + (1,) * (len(dims) - dim - 1))

    factor_of = one(*cuts[0])
    for cut in cuts[1:]:
        factor_of = factor_of * one(*cut)
    return factor_of


def routed_block(own_key, own, number, rows, count, top, limit, slope):
    ranking = jax.random.permutation(own_key, count)
    heavy_load, ordinary = shares(count, rows * top, limit, slope, True), shares(count, rows * top, limit, slope, False)
    places = jnp.arange(count)

    def named(lengths, offset_by):
        used = int((lengths > 0).sum())
        fixed = max(1, used // 4)
        shifted = fixed + (places - fixed + offset_by * (used - fixed)) % max(1, count - fixed)
        return jnp.zeros((count,), jnp.int32).at[ranking[jnp.where(places < fixed, places, shifted)]].set(jnp.asarray(lengths, jnp.int32))

    lengths = jnp.where(number % 4 == 0, named(heavy_load, number // 4), named(ordinary, number - number // 4 - 1))
    mixed = jax.random.permutation(jax.random.fold_in(own, 3), count)
    source_of, taker = mixed[0:count // 2 * 2:2], mixed[1:count // 2 * 2:2]
    margin = jnp.minimum(lengths[source_of] - 1, limit - lengths[taker]) // 2
    margin = jnp.where((source_of == ranking[0]) | (taker == ranking[0]) | (lengths[taker] == 0), 0, jnp.maximum(margin, 0))
    shifted = jax.random.randint(jax.random.fold_in(own, 4), (count // 2,), 0, 1 << 20) % (margin + 1)
    lengths = lengths.at[source_of].add(-shifted).at[taker].add(shifted)
    labels = jnp.searchsorted(jnp.cumsum(lengths), jnp.arange(rows * top), side="right").astype(jnp.int32)
    listing = labels.reshape(top, rows).T
    listing = listing[jax.random.permutation(jax.random.fold_in(own, 1), rows)]
    offset_by = jax.random.randint(jax.random.fold_in(own, 2), (rows, 1), 0, top)
    return jnp.take_along_axis(listing, (jnp.arange(top)[None, :] + offset_by) % top, axis=1)


def shares(amount, total, reach, lean, full):
    loads = [(1 << 20) // math.isqrt(standing ** lean) + 1 for standing in range(1, amount + 1)]
    largest = reach if full else min(reach, max(-(-total // amount), total * loads[0] // sum(loads)))
    least = 1 if total - largest >= amount - 1 else 0
    holding, surplus = [largest] + [least] * (amount - 1), total - largest - least * (amount - 1)
    while surplus > 0:
        free = [i for i in range(1, amount) if holding[i] < largest] or [i for i in range(1, amount) if holding[i] < reach]
        mass, left = sum([loads[i] for i in free]), surplus
        for i in free:
            extra = min(reach - holding[i], max(1, left * loads[i] // mass), surplus)
            holding[i] = holding[i] + extra
            surplus = surplus - extra
    return np.array(holding)


def noise(own_key, extent, scale, reach, cuts=(), held_as=jnp.bfloat16):
    values = jax.random.normal(own_key, extent, jnp.float32) * scale
    if len(cuts) > 0:
        values = block_levels(own_key, extent, cuts, -0.22, 0.18) * values
    return jnp.clip(values, min=-reach, max=reach).astype(held_as)


def setup_inputs(seed: int = 0) -> dict:
    keys = jax.random.split(jax.random.key(seed), 10)
    embeddings = noise(keys[0], (NODES, WIDTH), 1.0, 6.0, ((0, 128),))
    partition_source = draw_partition_source(jax.random.fold_in(keys[9], 71), 0)
    hash_target = draw_hash_target(jax.random.fold_in(keys[9], 71), 0)
    tile_values = noise(keys[3], (DEVICES * SLOTS, TILE, TILE), (TILE * SLOTS // ROW_BLOCKS) ** -0.5, 0.109375, ((0, 128),))
    tile_row = touch_ends(jax.random.randint(keys[4], (DEVICES * SLOTS,), 0, ROW_BLOCKS), jax.random.fold_in(keys[4], 1), 0, ROW_BLOCKS - 1).astype(jnp.int32)
    tile_owner_keys = jax.random.split(jax.random.fold_in(keys[5], 1), (DEVICES * SLOTS) // SLOTS)
    tile_owner_turns = jax.random.permutation(jax.random.fold_in(keys[5], 3), (DEVICES * SLOTS) // SLOTS)
    tile_owner = jax.vmap(lambda own, number: routed_block(jax.random.fold_in(keys[5], 2), own, number, SLOTS, N_COL, 1, OWNER_CAP, 1))(tile_owner_keys, tile_owner_turns).reshape((DEVICES * SLOTS, 1))
    tile_sub = touch_ends(jax.random.randint(keys[6], (DEVICES * SLOTS,), 0, ROW_BLOCKS), jax.random.fold_in(keys[6], 1), 0, ROW_BLOCKS - 1).astype(jnp.int32)
    tile_count = draw_tile_count(jax.random.fold_in(keys[9], 71), 0)
    cotangent = noise(keys[8], (NODES, WIDTH), 1.0, 6.0, ((0, 128),))
    return {"embeddings": embeddings, "partition_source": partition_source, "hash_target": hash_target, "tile_values": tile_values, "tile_row": tile_row, "tile_owner": tile_owner, "tile_sub": tile_sub, "tile_count": tile_count, "cotangent": cotangent}


PRECISE = lax.Precision.HIGHEST


def spread_device(values, rows, columns, live_slots, group_rows):
    blocks = group_rows.reshape(-1, TILE, WIDTH)[columns]
    products = jnp.einsum("sij,sjw->siw", values.astype(jnp.float32), blocks.astype(jnp.float32), precision=PRECISE)
    selector = (rows[None, :] == jnp.arange(NODES_DEV // TILE, dtype=jnp.int32)[:, None]).astype(jnp.float32) * live_slots[None, :]
    summed = jnp.einsum("bs,siw->biw", selector, products, precision=PRECISE)
    return summed.reshape(NODES_DEV, WIDTH)


def spread(features, values, rows, columns, live_slots):
    span = NODES_DEV * N_COL

    def per_device(index):
        group_rows = lax.dynamic_slice_in_dim(features, (index // N_COL) * span, span, 0)
        return spread_device(values[index], rows[index], columns[index], live_slots[index], group_rows)

    return lax.map(per_device, jnp.arange(DEVICES, dtype=jnp.int32)).reshape(-1, WIDTH)


def back_device(values, rows, columns, live_slots, local_rows):
    chosen = local_rows.reshape(-1, TILE, WIDTH)[rows]
    products = jnp.einsum("sij,siw->sjw", values.astype(jnp.float32), chosen.astype(jnp.float32), precision=PRECISE)
    products = products * live_slots[:, None, None]
    partial_sum = jax.ops.segment_sum(products, columns, num_segments=N_COL * (NODES_DEV // TILE))
    rounded = lax.optimization_barrier(partial_sum.astype(jnp.bfloat16)).astype(jnp.float32)
    return rounded.reshape(-1, WIDTH)


def transpose_apply(gradient, values, rows, columns, live_slots):
    span = NODES_DEV * N_COL

    def per_group(group_index):
        def accumulate(running, col_index):
            index = group_index * N_COL + col_index
            local_rows = lax.dynamic_slice_in_dim(gradient, index * NODES_DEV, NODES_DEV, 0)
            term = back_device(values[index], rows[index], columns[index], live_slots[index], local_rows)
            return running + term, None

        running, _ = lax.scan(accumulate, jnp.zeros((span, WIDTH), jnp.float32), jnp.arange(N_COL, dtype=jnp.int32))
        return running

    return lax.map(per_group, jnp.arange(N_ROW, dtype=jnp.int32)).reshape(-1, WIDTH)


def reference(embeddings, partition_source, hash_target, tile_values, tile_row, tile_owner, tile_sub, tile_count, cotangent):
    values = tile_values.reshape(DEVICES, SLOTS, TILE, TILE)
    rows = tile_row.reshape(DEVICES, SLOTS)
    columns = (tile_owner[:, 0] * (NODES_DEV // TILE) + tile_sub).reshape(DEVICES, SLOTS)
    live_slots = (jnp.arange(SLOTS, dtype=jnp.int32)[None, :] < tile_count[:, None]).astype(jnp.float32)
    initial = embeddings[partition_source]
    layer_one = spread(initial, values, rows, columns, live_slots).astype(jnp.bfloat16)
    layer_one = lax.optimization_barrier(layer_one)
    layer_two = spread(layer_one, values, rows, columns, live_slots)
    propagated = ((initial.astype(jnp.float32) + layer_one.astype(jnp.float32) + layer_two) / 3.0).astype(jnp.bfloat16)
    back_one = transpose_apply(cotangent, values, rows, columns, live_slots)
    middle = ((cotangent.astype(jnp.float32) + back_one) / 3.0).astype(jnp.bfloat16)
    back_zero = transpose_apply(middle, values, rows, columns, live_slots)
    grad_part = (cotangent.astype(jnp.float32) / 3.0 + back_zero).astype(jnp.bfloat16)
    return propagated, grad_part[hash_target]
```

```python
import functools

import jax
import jax.numpy as jnp
from jax import lax
from jax.experimental import pallas as pl
from jax.experimental.pallas import tpu as pltpu
from jax.sharding import PartitionSpec as P

SIDE = 4
CORES = 2
TILE = 128
NODES = 512
HALF = 256
WIDTH = 256
GROUP = SIDE * HALF
SLOTS = 96
BF16 = jnp.bfloat16
F32 = jnp.float32
VMEM_LIMIT = 48 * 1024 * 1024

WHOLE = pl.BlockSpec(memory_space=pltpu.VMEM)


def params(limit=VMEM_LIMIT):
    return pltpu.CompilerParams(vmem_limit_bytes=limit)


def struct(shape, dtype):
    return jax.ShapeDtypeStruct(shape, dtype)


def cost(flops, nbytes):
    return pl.CostEstimate(flops=int(flops), bytes_accessed=int(nbytes), transcendentals=0)


def move(array, axis, step):
    pairs = []
    for x in range(SIDE):
        for y in range(SIDE):
            for c in range(CORES):
                to_x = (x + step) % SIDE if axis == "x" else x
                to_y = (y + step) % SIDE if axis == "y" else y
                to_c = (c + step) % CORES if axis == "c" else c
                pairs.append(((x * SIDE + y) * CORES + c, (to_x * SIDE + to_y) * CORES + to_c))
    return lax.ppermute(array, "col", pairs)


def reshuffle(payload):
    devices = lax.axis_size("row") * lax.axis_size("col")
    direct = payload.reshape(devices, NODES // devices, WIDTH)
    moved = lax.all_to_all(direct, ("row", "col"), split_axis=0, concat_axis=0, tiled=True)
    return moved.reshape(payload.shape)


def order_kernel(transposed, key_row, key_col, data, out):
    below = (key_col[...] < key_row[...]).astype(jnp.int32)
    rank = jnp.sum(below, axis=0, keepdims=True)
    spot = lax.broadcasted_iota(jnp.int32, (NODES, NODES), 0)
    select = (spot == rank).astype(F32).astype(BF16)
    dims = (((1,), (1 if transposed else 0,)), ((), ()))
    out[...] = lax.dot_general(select, data[...], dims, preferred_element_type=F32).astype(BF16)


def restore_kernel(key_row, key_col, data, out):
    below = (key_row[...] < key_col[...]).astype(jnp.int32)
    rank = jnp.sum(below, axis=1, keepdims=True)
    spot = lax.broadcasted_iota(jnp.int32, (NODES, NODES), 1)
    select = (spot == rank).astype(F32).astype(BF16)
    out[...] = jnp.dot(select, data[...], preferred_element_type=F32).astype(BF16)


def permute_call(kernel, key, data):
    return pl.pallas_call(
        kernel,
        out_shape=struct((NODES, WIDTH), BF16),
        in_specs=[WHOLE] * 3,
        out_specs=WHOLE,
        compiler_params=params(),
        cost_estimate=cost(2 * NODES * NODES * WIDTH, 4 * NODES * WIDTH),
    )(key.reshape(1, NODES), key.reshape(NODES, 1), data)


def build_kernel(group, row, col, tiles, out, listed, counts):
    step = pl.program_id(0)

    @pl.when(step == 0)
    def _():
        for g in range(2 * SIDE + 1):
            counts[g] = 0

        def note(s, carry):
            g = group[s]
            n = counts[g]
            listed[g * SLOTS + n] = s
            counts[g] = n + 1
            return carry

        lax.fori_loop(0, SLOTS, note, 0)

    out[...] = jnp.zeros(out.shape, BF16)

    def place(n, carry):
        s = listed[step * SLOTS + n]
        rows = pl.ds(pl.multiple_of(row[s] * TILE, TILE), TILE)
        cols = pl.ds(pl.multiple_of(col[s] * TILE, TILE), TILE)
        held = out[0, rows, cols].astype(F32) + tiles[s].astype(F32)
        out[0, rows, cols] = held.astype(BF16)
        return carry

    lax.fori_loop(0, counts[step], place, 0)


def build(tiles, group, row, col):
    return pl.pallas_call(
        build_kernel,
        out_shape=struct((2 * SIDE, NODES, GROUP), BF16),
        grid_spec=pltpu.PrefetchScalarGridSpec(
            num_scalar_prefetch=3,
            grid=(2 * SIDE,),
            in_specs=[WHOLE],
            out_specs=pl.BlockSpec((1, NODES, GROUP), lambda i, *_: (i, 0, 0)),
            scratch_shapes=[
                pltpu.SMEM(((2 * SIDE + 1) * SLOTS,), jnp.int32),
                pltpu.SMEM((2 * SIDE + 1,), jnp.int32),
            ],
        ),
        compiler_params=params(),
        cost_estimate=cost(1e6, 14e6),
    )(group, row, col, tiles)


def step_group(groups, i):
    at = groups[-1]
    for k in range(len(groups) - 2, -1, -1):
        at = jnp.where(i == k, groups[k], at)
    return at


def matrix_spec(groups):
    return pl.BlockSpec((1, NODES, GROUP), lambda i: (step_group(groups, i), 0, 0))


def forward_kernel(count, seeded, last, own, peer, *refs):
    pieces, refs = refs[:count], refs[count:]
    if seeded:
        seed_own, seed_peer, refs = refs[0], refs[1], refs[2:]
    out_own, out_peer, acc_own, acc_peer = refs
    step = pl.program_id(0)

    @pl.when(step == 0)
    def _():
        acc_own[...] = seed_own[...] if seeded else jnp.zeros(acc_own.shape, F32)
        acc_peer[...] = seed_peer[...] if seeded else jnp.zeros(acc_peer.shape, F32)

    for k in range(count):

        @pl.when(step == k)
        def _(k=k):
            acc_own[...] += jnp.dot(own[0], pieces[k][...], preferred_element_type=F32)
            acc_peer[...] += jnp.dot(peer[0], pieces[k][...], preferred_element_type=F32)

    @pl.when(step == count - 1)
    def _():
        out_own[...] = acc_own[...]
        out_peer[...] = acc_peer[...].astype(out_peer.dtype)


def forward_product(matrices, groups, pieces, seeds, last):
    shape = (NODES, WIDTH)
    count = len(groups)
    return pl.pallas_call(
        functools.partial(forward_kernel, count, seeds is not None, last),
        grid=(count,),
        out_shape=(struct(shape, F32), struct(shape, BF16 if last else F32)),
        in_specs=[matrix_spec(groups)] * 2 + [WHOLE] * (count + (2 if seeds else 0)),
        out_specs=(WHOLE, WHOLE),
        scratch_shapes=[pltpu.VMEM(shape, F32), pltpu.VMEM(shape, F32)],
        compiler_params=params(),
        cost_estimate=cost(count * 4 * NODES * GROUP * WIDTH, count * 4 * NODES * GROUP),
    )(*matrices, *pieces, *(seeds or ()))


def backward_kernel(count, parts, own, peer, mine, theirs, *outs):
    step = pl.program_id(0)
    for k in range(count):

        @pl.when(step == k)
        def _(k=k):
            for d in range(SIDE):
                cols = slice(d * HALF, (d + 1) * HALF)
                got = jnp.dot(mine[...], own[0, :, cols], preferred_element_type=F32)
                got += jnp.dot(theirs[...], peer[0, :, cols], preferred_element_type=F32)
                out = outs[k * parts + d * parts // SIDE]
                out[d % (SIDE // parts)] = got.astype(out.dtype)


def backward_product(matrices, groups, mine, theirs, parts, dtype):
    count = len(groups)
    outs = [struct((SIDE // parts, WIDTH, HALF), dtype)] * (count * parts)
    return pl.pallas_call(
        functools.partial(backward_kernel, count, parts),
        grid=(count,),
        out_shape=outs,
        in_specs=[matrix_spec(groups)] * 2 + [WHOLE] * 2,
        out_specs=[WHOLE] * len(outs),
        compiler_params=params(),
        cost_estimate=cost(count * 4 * NODES * GROUP * WIDTH, count * 4 * NODES * GROUP),
    )(*matrices, mine, theirs)


AXES = (("x", "y"), ("y", "x"))


def spread(features, matrices):
    first, late = [], []
    for h in range(2):
        short, long = AXES[h]
        shard = features[h * HALF : (h + 1) * HALF]
        line = [shard, move(shard, short, -1), move(shard, short, 2), move(shard, short, 1)]
        line = jnp.concatenate(line, axis=0)
        up, down = move(line, long, -1), move(line, long, 1)
        first.append((line, up, down))
    for h in range(2):
        long = AXES[h][1]
        line, up, down = first[h]
        late.append((move(down[: GROUP // 2], long, 1), move(up[GROUP // 2 :], long, -1)))
    sums = forward_product(
        matrices, (0, 1, 3, 4, 5, 7), [piece for half in first for piece in half], None, False
    )
    ends = [jnp.concatenate(pair, axis=0) for pair in late]
    own, peer = forward_product(matrices, (2, 6), ends, sums, True)
    return own + move(peer, "c", 1).astype(F32)


def collect(mine, theirs, matrices):
    far = backward_product(matrices, (2, 6), mine, theirs, 2, BF16)
    near = backward_product(matrices, (1, 3, 5, 7), mine, theirs, 1, F32)
    here = backward_product(matrices, (0, 4), mine, theirs, 1, F32)
    passed = []
    for h in range(2):
        long = AXES[h][1]
        passed.append((move(far[2 * h], long, 1), move(far[2 * h + 1], long, -1)))
    half = SIDE // 2
    arrived = []
    for h in range(2):
        long = AXES[h][1]
        up, down = near[2 * h], near[2 * h + 1]
        low, high = passed[h]
        up = jnp.concatenate([up[:half] + low.astype(F32), up[half:]], axis=0).astype(BF16)
        down = jnp.concatenate([down[:half], down[half:] + high.astype(F32)], axis=0).astype(BF16)
        arrived.append((move(up, long, 1), move(down, long, -1)))
    sums = []
    for h in range(2):
        short = AXES[h][0]
        low, high = arrived[h]
        line = here[h] + low.astype(F32) + high.astype(F32)
        sent = line.astype(BF16)
        total = line[0] + move(sent[1], short, 1).astype(F32)
        total += move(sent[2], short, 2).astype(F32) + move(sent[3], short, -1).astype(F32)
        sums.append(total)
    return jnp.concatenate(sums, axis=1)


def shards(
    embeddings,
    partition_source,
    hash_target,
    tile_values,
    tile_row,
    tile_owner,
    tile_sub,
    tile_count,
    cotangent,
):
    index = lax.axis_index("col")
    core = index % CORES
    own_y = (index // CORES) % SIDE
    own_x = index // (CORES * SIDE)

    peer_tiles = move(tile_values, "c", 1)
    live = jnp.arange(SLOTS, dtype=jnp.int32) < tile_count[0]
    owner = tile_owner[:, 0]
    meta = jnp.stack([jnp.where(live, owner, -1), tile_row, tile_sub])
    peer_meta = move(meta, "c", 1)

    def place(meta):
        owner, row, sub = meta[0], meta[1], meta[2]
        far_x = (owner // (CORES * SIDE) - own_x) % SIDE
        far_y = (owner // CORES - own_y) % SIDE
        used = (owner >= 0) & (owner % CORES == core)
        first = sub < 2
        group = jnp.where(used, jnp.where(first, far_y, SIDE + far_x), 2 * SIDE)
        return group, row, jnp.where(first, far_x, far_y) * 2 + sub % 2

    matrices = (build(tile_values, *place(meta)), build(peer_tiles, *place(peer_meta)))

    part_key = (partition_source // NODES) * NODES + jnp.arange(NODES, dtype=jnp.int32)
    order = functools.partial(order_kernel, False)
    incoming = reshuffle(permute_call(order, hash_target, embeddings))
    initial = permute_call(restore_kernel, part_key, incoming)
    layer_one = spread(initial, matrices).astype(BF16)
    layer_two = spread(layer_one, matrices)
    propagated = ((initial.astype(F32) + layer_one.astype(F32) + layer_two) / 3.0).astype(BF16)

    turned = cotangent.T
    back_one = collect(turned, move(turned, "c", 1), matrices)
    middle = ((turned.astype(F32) + back_one) / 3.0).astype(BF16)
    back_zero = collect(middle, move(middle, "c", 1), matrices)
    grad_part = (turned.astype(F32) / 3.0 + back_zero).astype(BF16)
    order = functools.partial(order_kernel, True)
    returned = reshuffle(permute_call(order, part_key, grad_part))
    embed_grad = permute_call(restore_kernel, hash_target, returned)
    return propagated, embed_grad


def solution(mesh):
    both = ("row", "col")
    return jax.shard_map(
        shards,
        mesh=mesh,
        in_specs=(
            P(both, None),
            P(both),
            P(both),
            P(both, None, None),
            P(both),
            P(both, None),
            P(both),
            P(both),
            P(both, None),
        ),
        out_specs=(P(both, None), P(both, None)),
        check_vma=False,
    )
```

```python
import functools

import jax
import jax.numpy as jnp
from jax import lax
from jax.experimental import pallas as pl
from jax.experimental.pallas import tpu as pltpu
from jax.sharding import PartitionSpec as P

SIDE = 4
CORES = 2
TILE = 128
NODES = 512
BLOCKS = NODES // TILE
WIDTH = 256
SLOTS = 96
OWNER_CAP = 4
CAP = SIDE * CORES * OWNER_CAP
CODE_ROWS = 16
COUNT_LANE = 64
PACKED = CAP * TILE + CODE_ROWS
COLUMNS = CORES * SIDE * BLOCKS
TURNED = BLOCKS * WIDTH
BF16 = jnp.bfloat16
F32 = jnp.float32
VMEM_LIMIT = 48 * 1024 * 1024

WHOLE = pl.BlockSpec(memory_space=pltpu.VMEM)
SCALARS = pl.BlockSpec(memory_space=pltpu.SMEM)


def params(limit=VMEM_LIMIT):
    return pltpu.CompilerParams(vmem_limit_bytes=limit)


def struct(shape, dtype):
    return jax.ShapeDtypeStruct(shape, dtype)


def cost(flops, nbytes):
    return pl.CostEstimate(flops=int(flops), bytes_accessed=int(nbytes), transcendentals=0)


def move(array, axis, step):
    pairs = []
    for x in range(SIDE):
        for y in range(SIDE):
            for c in range(CORES):
                to_x = (x + step) % SIDE if axis == "x" else x
                to_y = (y + step) % SIDE if axis == "y" else y
                to_c = (c + step) % CORES if axis == "c" else c
                pairs.append(((x * SIDE + y) * CORES + c, (to_x * SIDE + to_y) * CORES + to_c))
    return lax.ppermute(array, "col", pairs)


def reshuffle(payload):
    devices = lax.axis_size("row") * lax.axis_size("col")
    direct = payload.reshape(devices, NODES // devices, WIDTH)
    moved = lax.all_to_all(direct, ("row", "col"), split_axis=0, concat_axis=0, tiled=True)
    return moved.reshape(payload.shape)


def ordering(key_row, key_col):
    below = (key_col[...] < key_row[...]).astype(jnp.int32)
    rank = jnp.sum(below, axis=0, keepdims=True)
    spot = lax.broadcasted_iota(jnp.int32, (NODES, NODES), 0)
    return (spot == rank).astype(F32).astype(BF16)


def order_kernel(key_row, key_col, data, out):
    select = ordering(key_row, key_col)
    out[...] = jnp.dot(select, data[...], preferred_element_type=F32).astype(BF16)


def order_turned_kernel(key_row, key_col, data, out):
    select = ordering(key_row, key_col)
    total = jnp.zeros((NODES, WIDTH), F32)
    for b in range(BLOCKS):
        part = select[:, b * TILE : (b + 1) * TILE]
        block = data[b * WIDTH : (b + 1) * WIDTH, :]
        total += lax.dot_general(part, block, (((1,), (1,)), ((), ())), preferred_element_type=F32)
    out[...] = total.astype(BF16)


def restore_kernel(key_row, key_col, data, out):
    below = (key_row[...] < key_col[...]).astype(jnp.int32)
    rank = jnp.sum(below, axis=1, keepdims=True)
    spot = lax.broadcasted_iota(jnp.int32, (NODES, NODES), 1)
    select = (spot == rank).astype(F32).astype(BF16)
    out[...] = jnp.dot(select, data[...], preferred_element_type=F32).astype(BF16)


def permute_call(kernel, key, data):
    return pl.pallas_call(
        kernel,
        out_shape=struct((NODES, WIDTH), BF16),
        in_specs=[WHOLE] * 3,
        out_specs=WHOLE,
        compiler_params=params(),
        cost_estimate=cost(2 * NODES * NODES * WIDTH, 4 * NODES * WIDTH),
    )(key.reshape(1, NODES), key.reshape(NODES, 1), data)


def bucket_kernel(target, code, tiles, *refs):
    outs, (listed, counts) = refs[:SIDE], refs[SIDE:]
    for d in range(SIDE + 1):
        counts[d] = 0

    def note(s, carry):
        d = target[s]
        n = counts[d]
        listed[d * SLOTS + n] = s
        counts[d] = n + 1
        return carry

    lax.fori_loop(0, SLOTS, note, 0)
    lane = lax.broadcasted_iota(jnp.int32, (CODE_ROWS, TILE), 1)
    for d in range(SIDE):
        used = counts[d]

        def place(n, codes, d=d):
            s = listed[d * SLOTS + n]
            outs[d][pl.ds(pl.multiple_of(n * TILE, TILE), TILE), :] = tiles[s]
            return jnp.where(lane == n, code[s], codes)

        def clear(n, carry, d=d):
            outs[d][pl.ds(pl.multiple_of(n * TILE, TILE), TILE), :] = jnp.zeros((TILE, TILE), BF16)
            return carry

        codes = lax.fori_loop(0, used, place, jnp.zeros((CODE_ROWS, TILE), jnp.int32))
        lax.fori_loop(used, CAP, clear, 0)
        codes = jnp.where(lane == COUNT_LANE, used, codes)
        outs[d][CAP * TILE :, :] = codes.astype(F32).astype(BF16)


def bucket(tiles, target, code):
    return pl.pallas_call(
        bucket_kernel,
        out_shape=[struct((PACKED, TILE), BF16)] * SIDE,
        in_specs=[SCALARS, SCALARS, WHOLE],
        out_specs=[WHOLE] * SIDE,
        scratch_shapes=[
            pltpu.SMEM(((SIDE + 1) * SLOTS,), jnp.int32),
            pltpu.SMEM((SIDE + 1,), jnp.int32),
        ],
        compiler_params=params(),
        cost_estimate=cost(1e6, 7e6),
    )(target, code, tiles)


def slot_steps(codes):
    most = codes[COUNT_LANE]
    for k in range(1, SIDE):
        most = jnp.maximum(most, codes[k * TILE + COUNT_LANE])
    return (most + 1) // 2


def forward_kernel(codes, *refs):
    tiles, refs = refs[:SIDE], refs[SIDE:]
    shards, refs = refs[: CORES * SIDE], refs[CORES * SIDE :]
    outs, (features, *totals) = refs[:SIDE], refs[SIDE:]
    for j in range(CORES * SIDE):
        features[j * NODES : (j + 1) * NODES, :] = shards[j][...]
    for k in range(SIDE):
        totals[k][...] = jnp.zeros((NODES, WIDTH), F32)

    def step(i, carry):
        for u in range(2):
            n = i * 2 + u
            for k in range(SIDE):
                code = codes[k * TILE + n]
                row = pl.multiple_of((code // COLUMNS) * TILE, TILE)
                column = pl.multiple_of((code % COLUMNS) * TILE, TILE)
                tile = tiles[k][pl.ds(pl.multiple_of(n * TILE, TILE), TILE), :]
                block = features[pl.ds(column, TILE), :]
                totals[k][pl.ds(row, TILE), :] += jnp.dot(tile, block, preferred_element_type=F32)
        return carry

    lax.fori_loop(0, slot_steps(codes), step, 0)
    for k in range(SIDE):
        outs[k][...] = totals[k][...].astype(outs[k].dtype)


def forward_product(packs, codes, shards):
    shape = (NODES, WIDTH)
    return pl.pallas_call(
        forward_kernel,
        out_shape=[struct(shape, F32)] + [struct(shape, BF16)] * (SIDE - 1),
        in_specs=[SCALARS] + [WHOLE] * (SIDE + CORES * SIDE),
        out_specs=[WHOLE] * SIDE,
        scratch_shapes=[pltpu.VMEM((CORES * SIDE * NODES, WIDTH), BF16)]
        + [pltpu.VMEM(shape, F32)] * SIDE,
        compiler_params=params(),
        cost_estimate=cost(1e9, 16e6),
    )(codes, *packs, *shards)


def backward_kernel(codes, *refs):
    tiles, refs = refs[:SIDE], refs[SIDE:]
    shards, refs = refs[:SIDE], refs[SIDE:]
    outs, (totals,) = refs[: CORES * SIDE], refs[CORES * SIDE :]
    totals[...] = jnp.zeros(totals.shape, F32)

    def step(i, carry):
        for u in range(2):
            n = i * 2 + u
            for k in range(SIDE):
                code = codes[k * TILE + n]
                row = pl.multiple_of((code // COLUMNS) * WIDTH, WIDTH)
                column = pl.multiple_of((code % COLUMNS) * WIDTH, WIDTH)
                tile = tiles[k][pl.ds(pl.multiple_of(n * TILE, TILE), TILE), :]
                block = shards[k][pl.ds(row, WIDTH), :]
                totals[pl.ds(column, WIDTH), :] += jnp.dot(block, tile, preferred_element_type=F32)
        return carry

    lax.fori_loop(0, slot_steps(codes), step, 0)
    for j in range(CORES * SIDE):
        outs[j][...] = totals[j * TURNED : (j + 1) * TURNED, :].astype(outs[j].dtype)


def backward_product(packs, codes, shards):
    shape = (TURNED, TILE)
    return pl.pallas_call(
        backward_kernel,
        out_shape=[struct(shape, F32)] * SIDE + [struct(shape, BF16)] * SIDE,
        in_specs=[SCALARS] + [WHOLE] * (2 * SIDE),
        out_specs=[WHOLE] * (CORES * SIDE),
        scratch_shapes=[pltpu.VMEM((CORES * SIDE * TURNED, TILE), F32)],
        compiler_params=params(),
        cost_estimate=cost(1e9, 16e6),
    )(codes, *packs, *shards)


ORDER = (2, 1, 3)


def gather_line(array, axis):
    got = {d: move(array, axis, d) for d in ORDER}
    return [array] + [got[d] for d in range(1, SIDE)]


def gather_forward(features):
    line = gather_line(features, "x")
    return line + [move(shard, "c", 1) for shard in line]


def scatter_forward(terms):
    total = terms[0]
    got = {k: move(terms[k], "y", -k) for k in ORDER}
    for k in ORDER:
        total = total + got[k].astype(F32)
    return total


def scatter_backward(terms):
    near, far = terms[:SIDE], terms[SIDE:]
    got = {}
    for j in ORDER:
        both = near[j] + move(far[j], "c", 1).astype(F32)
        got[j] = move(both.astype(BF16), "x", -j)
    total = near[0] + move(far[0], "c", 1).astype(F32)
    for j in ORDER:
        total = total + got[j].astype(F32)
    return total


def shards(
    embeddings,
    partition_source,
    hash_target,
    tile_values,
    tile_row,
    tile_owner,
    tile_sub,
    tile_count,
    cotangent,
):
    index = lax.axis_index("col")
    core = index % CORES
    own_y = (index // CORES) % SIDE
    own_x = index // (CORES * SIDE)

    owner = tile_owner[:, 0]
    live = jnp.arange(SLOTS, dtype=jnp.int32) < tile_count[0]
    back_x = (own_x - owner // (CORES * SIDE)) % SIDE
    far_y = (owner // CORES - own_y) % SIDE
    side = (owner + core) % CORES
    column = (side * SIDE + back_x) * BLOCKS + tile_sub
    target = jnp.where(live, far_y, SIDE)
    packs = bucket(tile_values, target, tile_row * COLUMNS + column)
    moved = {d: move(packs[d], "y", d) for d in ORDER}
    packs = [packs[0]] + [moved[d] for d in range(1, SIDE)]
    codes = jnp.concatenate([pack[CAP * TILE] for pack in packs]).astype(jnp.int32)

    part_key = (partition_source // NODES) * NODES + jnp.arange(NODES, dtype=jnp.int32)
    incoming = reshuffle(permute_call(order_kernel, hash_target, embeddings))
    initial = permute_call(restore_kernel, part_key, incoming)

    def spread(features):
        return scatter_forward(forward_product(packs, codes, gather_forward(features)))

    def collect(gradient):
        return scatter_backward(backward_product(packs, codes, gather_line(gradient, "y")))

    turned = cotangent.reshape(BLOCKS, TILE, WIDTH).transpose(0, 2, 1).reshape(TURNED, TILE)
    back_one = collect(turned)
    layer_one = spread(initial).astype(BF16)
    middle = ((turned.astype(F32) + back_one) / 3.0).astype(BF16)
    back_zero = collect(middle)
    layer_two = spread(layer_one)
    grad_part = (turned.astype(F32) / 3.0 + back_zero).astype(BF16)
    returned = reshuffle(permute_call(order_turned_kernel, part_key, grad_part))
    embed_grad = permute_call(restore_kernel, hash_target, returned)
    propagated = ((initial.astype(F32) + layer_one.astype(F32) + layer_two) / 3.0).astype(BF16)
    return propagated, embed_grad


def solution(mesh):
    both = ("row", "col")
    return jax.shard_map(
        shards,
        mesh=mesh,
        in_specs=(
            P(both, None),
            P(both),
            P(both),
            P(both, None, None),
            P(both),
            P(both, None),
            P(both),
            P(both),
            P(both, None),
        ),
        out_specs=(P(both, None), P(both, None)),
        check_vma=False,
    )
```

```python
import functools

import jax
import jax.numpy as jnp
from jax import lax
from jax.experimental import pallas as pl
from jax.experimental.pallas import tpu as pltpu
from jax.sharding import PartitionSpec as P

SIDE = 4
CORES = 2
TILE = 128
NODES = 512
BLOCKS = NODES // TILE
WIDTH = 256
SLOTS = 96
OWNER_CAP = 4
CAP = SIDE * CORES * OWNER_CAP
CODE_ROWS = 16
COUNT_LANE = 64
PACKED = CAP * TILE + CODE_ROWS
COLUMNS = CORES * SIDE * BLOCKS
TURNED = BLOCKS * WIDTH
BF16 = jnp.bfloat16
F32 = jnp.float32
VMEM_LIMIT = 48 * 1024 * 1024

WHOLE = pl.BlockSpec(memory_space=pltpu.VMEM)
SCALARS = pl.BlockSpec(memory_space=pltpu.SMEM)


def params(limit=VMEM_LIMIT):
    return pltpu.CompilerParams(vmem_limit_bytes=limit)


def struct(shape, dtype):
    return jax.ShapeDtypeStruct(shape, dtype)


def cost(flops, nbytes):
    return pl.CostEstimate(flops=int(flops), bytes_accessed=int(nbytes), transcendentals=0)


def move(array, axis, step):
    pairs = []
    for x in range(SIDE):
        for y in range(SIDE):
            for c in range(CORES):
                to_x = (x + step) % SIDE if axis == "x" else x
                to_y = (y + step) % SIDE if axis == "y" else y
                to_c = (c + step) % CORES if axis == "c" else c
                pairs.append(((x * SIDE + y) * CORES + c, (to_x * SIDE + to_y) * CORES + to_c))
    return lax.ppermute(array, "col", pairs)


def reshuffle(payload):
    devices = lax.axis_size("row") * lax.axis_size("col")
    direct = payload.reshape(devices, NODES // devices, WIDTH)
    moved = lax.all_to_all(direct, ("row", "col"), split_axis=0, concat_axis=0, tiled=True)
    return moved.reshape(payload.shape)


def ordering(key_row, key_col):
    below = (key_col[...] < key_row[...]).astype(jnp.int32)
    rank = jnp.sum(below, axis=0, keepdims=True)
    spot = lax.broadcasted_iota(jnp.int32, (NODES, NODES), 0)
    return (spot == rank).astype(F32).astype(BF16)


def order_kernel(key_row, key_col, data, out):
    select = ordering(key_row, key_col)
    out[...] = jnp.dot(select, data[...], preferred_element_type=F32).astype(BF16)


def order_turned_kernel(key_row, key_col, data, out):
    select = ordering(key_row, key_col)
    total = jnp.zeros((NODES, WIDTH), F32)
    for b in range(BLOCKS):
        part = select[:, b * TILE : (b + 1) * TILE]
        block = data[b * WIDTH : (b + 1) * WIDTH, :]
        total += lax.dot_general(part, block, (((1,), (1,)), ((), ())), preferred_element_type=F32)
    out[...] = total.astype(BF16)


def restore_kernel(key_row, key_col, data, out):
    below = (key_row[...] < key_col[...]).astype(jnp.int32)
    rank = jnp.sum(below, axis=1, keepdims=True)
    spot = lax.broadcasted_iota(jnp.int32, (NODES, NODES), 1)
    select = (spot == rank).astype(F32).astype(BF16)
    out[...] = jnp.dot(select, data[...], preferred_element_type=F32).astype(BF16)


def permute_call(kernel, key, data):
    return pl.pallas_call(
        kernel,
        out_shape=struct((NODES, WIDTH), BF16),
        in_specs=[WHOLE] * 3,
        out_specs=WHOLE,
        compiler_params=params(),
        cost_estimate=cost(2 * NODES * NODES * WIDTH, 4 * NODES * WIDTH),
    )(key.reshape(1, NODES), key.reshape(NODES, 1), data)


def bucket_kernel(target, code, tiles, *refs):
    outs, (listed, counts) = refs[:SIDE], refs[SIDE:]
    for d in range(SIDE + 1):
        counts[d] = 0

    def note(s, carry):
        d = target[s]
        n = counts[d]
        listed[d * SLOTS + n] = s
        counts[d] = n + 1
        return carry

    lax.fori_loop(0, SLOTS, note, 0)
    lane = lax.broadcasted_iota(jnp.int32, (CODE_ROWS, TILE), 1)
    for d in range(SIDE):
        used = counts[d]

        def place(n, codes, d=d):
            s = listed[d * SLOTS + n]
            outs[d][pl.ds(pl.multiple_of(n * TILE, TILE), TILE), :] = tiles[s]
            return jnp.where(lane == n, code[s], codes)

        def clear(n, carry, d=d):
            outs[d][pl.ds(pl.multiple_of(n * TILE, TILE), TILE), :] = jnp.zeros((TILE, TILE), BF16)
            return carry

        codes = lax.fori_loop(0, used, place, jnp.zeros((CODE_ROWS, TILE), jnp.int32))
        lax.fori_loop(used, CAP, clear, 0)
        codes = jnp.where(lane == COUNT_LANE, used, codes)
        outs[d][CAP * TILE :, :] = codes.astype(F32).astype(BF16)


def bucket(tiles, target, code):
    return pl.pallas_call(
        bucket_kernel,
        out_shape=[struct((PACKED, TILE), BF16)] * SIDE,
        in_specs=[SCALARS, SCALARS, WHOLE],
        out_specs=[WHOLE] * SIDE,
        scratch_shapes=[
            pltpu.SMEM(((SIDE + 1) * SLOTS,), jnp.int32),
            pltpu.SMEM((SIDE + 1,), jnp.int32),
        ],
        compiler_params=params(),
        cost_estimate=cost(1e6, 7e6),
    )(target, code, tiles)


def slot_steps(codes):
    most = codes[COUNT_LANE]
    for k in range(1, SIDE):
        most = jnp.maximum(most, codes[k * TILE + COUNT_LANE])
    return (most + 1) // 2


def product_kernel(codes, *refs):
    tiles, refs = refs[:SIDE], refs[SIDE:]
    shards, refs = refs[: CORES * SIDE], refs[CORES * SIDE :]
    turned, refs = refs[:SIDE], refs[SIDE:]
    rows_out, refs = refs[:SIDE], refs[SIDE:]
    columns_out, (features, columns, *rows) = refs[: CORES * SIDE], refs[CORES * SIDE :]
    for j in range(CORES * SIDE):
        features[j * NODES : (j + 1) * NODES, :] = shards[j][...]
    columns[...] = jnp.zeros(columns.shape, F32)
    for k in range(SIDE):
        rows[k][...] = jnp.zeros((NODES, WIDTH), F32)

    def step(i, carry):
        for u in range(2):
            n = i * 2 + u
            for k in range(SIDE):
                code = codes[k * TILE + n]
                row, column = code // COLUMNS, code % COLUMNS
                tile = tiles[k][pl.ds(pl.multiple_of(n * TILE, TILE), TILE), :]
                block = features[pl.ds(pl.multiple_of(column * TILE, TILE), TILE), :]
                to = pl.ds(pl.multiple_of(row * TILE, TILE), TILE)
                rows[k][to, :] += jnp.dot(tile, block, preferred_element_type=F32)
                block = turned[k][pl.ds(pl.multiple_of(row * WIDTH, WIDTH), WIDTH), :]
                to = pl.ds(pl.multiple_of(column * WIDTH, WIDTH), WIDTH)
                columns[to, :] += jnp.dot(block, tile, preferred_element_type=F32)
        return carry

    lax.fori_loop(0, slot_steps(codes), step, 0)
    for k in range(SIDE):
        rows_out[k][...] = rows[k][...].astype(rows_out[k].dtype)
    for j in range(CORES * SIDE):
        part = columns[j * TURNED : (j + 1) * TURNED, :]
        columns_out[j][...] = part.astype(columns_out[j].dtype)


def products(packs, codes, shards, turned):
    plain, flipped = (NODES, WIDTH), (TURNED, TILE)
    outs = pl.pallas_call(
        product_kernel,
        out_shape=[struct(plain, F32)]
        + [struct(plain, BF16)] * (SIDE - 1)
        + [struct(flipped, F32)] * SIDE
        + [struct(flipped, BF16)] * SIDE,
        in_specs=[SCALARS] + [WHOLE] * (2 * SIDE + CORES * SIDE),
        out_specs=[WHOLE] * (SIDE + CORES * SIDE),
        scratch_shapes=[
            pltpu.VMEM((CORES * SIDE * NODES, WIDTH), BF16),
            pltpu.VMEM((CORES * SIDE * TURNED, TILE), F32),
        ]
        + [pltpu.VMEM(plain, F32)] * SIDE,
        compiler_params=params(),
        cost_estimate=cost(3e9, 16e6),
    )(codes, *packs, *shards, *turned)
    return outs[:SIDE], outs[SIDE:]


ORDER = (2, 1, 3)


def gather_line(array, axis):
    got = {d: move(array, axis, d) for d in ORDER}
    return [array] + [got[d] for d in range(1, SIDE)]


def gather_forward(features):
    line = gather_line(features, "x")
    return line + [move(shard, "c", 1) for shard in line]


def scatter_forward(terms):
    total = terms[0]
    got = {k: move(terms[k], "y", -k) for k in ORDER}
    for k in ORDER:
        total = total + got[k].astype(F32)
    return total


def scatter_backward(terms):
    near, far = terms[:SIDE], terms[SIDE:]
    got = {}
    for j in ORDER:
        both = near[j] + move(far[j], "c", 1).astype(F32)
        got[j] = move(both.astype(BF16), "x", -j)
    total = near[0] + move(far[0], "c", 1).astype(F32)
    for j in ORDER:
        total = total + got[j].astype(F32)
    return total


def shards(
    embeddings,
    partition_source,
    hash_target,
    tile_values,
    tile_row,
    tile_owner,
    tile_sub,
    tile_count,
    cotangent,
):
    index = lax.axis_index("col")
    core = index % CORES
    own_y = (index // CORES) % SIDE
    own_x = index // (CORES * SIDE)

    owner = tile_owner[:, 0]
    live = jnp.arange(SLOTS, dtype=jnp.int32) < tile_count[0]
    back_x = (own_x - owner // (CORES * SIDE)) % SIDE
    far_y = (owner // CORES - own_y) % SIDE
    side = (owner + core) % CORES
    column = (side * SIDE + back_x) * BLOCKS + tile_sub
    target = jnp.where(live, far_y, SIDE)
    turned = cotangent.reshape(BLOCKS, TILE, WIDTH).transpose(0, 2, 1).reshape(TURNED, TILE)
    gradients = gather_line(turned, "y")
    packs = bucket(tile_values, target, tile_row * COLUMNS + column)
    packs, gradients = lax.optimization_barrier((packs, gradients))
    moved = {d: move(packs[d], "y", d) for d in ORDER}
    packs = [packs[0]] + [moved[d] for d in range(1, SIDE)]
    codes = jnp.concatenate([pack[CAP * TILE] for pack in packs]).astype(jnp.int32)

    part_key = (partition_source // NODES) * NODES + jnp.arange(NODES, dtype=jnp.int32)
    incoming = reshuffle(permute_call(order_kernel, hash_target, embeddings))
    initial = permute_call(restore_kernel, part_key, incoming)

    rows, columns = products(packs, codes, gather_forward(initial), gradients)
    layer_one = scatter_forward(rows).astype(BF16)
    back_one = scatter_backward(columns)
    middle = ((turned.astype(F32) + back_one) / 3.0).astype(BF16)
    gradients = gather_line(middle, "y")
    rows, columns = products(packs, codes, gather_forward(layer_one), gradients)
    back_zero = scatter_backward(columns)
    layer_two = scatter_forward(rows)
    grad_part = (turned.astype(F32) / 3.0 + back_zero).astype(BF16)
    returned = reshuffle(permute_call(order_turned_kernel, part_key, grad_part))
    embed_grad = permute_call(restore_kernel, hash_target, returned)
    propagated = ((initial.astype(F32) + layer_one.astype(F32) + layer_two) / 3.0).astype(BF16)
    return propagated, embed_grad


def solution(mesh):
    both = ("row", "col")
    return jax.shard_map(
        shards,
        mesh=mesh,
        in_specs=(
            P(both, None),
            P(both),
            P(both),
            P(both, None, None),
            P(both),
            P(both, None),
            P(both),
            P(both),
            P(both, None),
        ),
        out_specs=(P(both, None), P(both, None)),
        check_vma=False,
    )
```

```python
import functools

import jax
import jax.numpy as jnp
from jax import lax
from jax.experimental import pallas as pl
from jax.experimental.pallas import tpu as pltpu
from jax.sharding import PartitionSpec as P

SIDE = 4
CORES = 2
TILE = 128
NODES = 512
BLOCKS = NODES // TILE
WIDTH = 256
SLOTS = 96
OWNER_CAP = 4
CAP = SIDE * CORES * OWNER_CAP
CODE_ROWS = 16
COUNT_LANE = 64
PACKED = CAP * TILE + CODE_ROWS
COLUMNS = CORES * SIDE * BLOCKS
TURNED = BLOCKS * WIDTH
PART = NODES // SIDE
SHIPPED = TURNED + PART * WIDTH // TILE
BF16 = jnp.bfloat16
F32 = jnp.float32
VMEM_LIMIT = 24 * 1024 * 1024
VMEM_MOST = 62 * 1024 * 1024

WHOLE = pl.BlockSpec(memory_space=pltpu.VMEM)
FAR = pl.BlockSpec(memory_space=pltpu.HBM)
SCALARS = pl.BlockSpec(memory_space=pltpu.SMEM)


def params(limit=VMEM_LIMIT):
    return pltpu.CompilerParams(vmem_limit_bytes=limit)


def struct(shape, dtype):
    return jax.ShapeDtypeStruct(shape, dtype)


def cost(flops, nbytes):
    return pl.CostEstimate(flops=int(flops), bytes_accessed=int(nbytes), transcendentals=0)


def move(array, axis, step):
    pairs = []
    for x in range(SIDE):
        for y in range(SIDE):
            for c in range(CORES):
                ahead = step * (1 - 2 * c)
                to_x = (x + ahead) % SIDE if axis == "x" else x
                to_y = (y + ahead) % SIDE if axis == "y" else y
                to_c = (c + step) % CORES if axis == "c" else c
                pairs.append(((x * SIDE + y) * CORES + c, (to_x * SIDE + to_y) * CORES + to_c))
    return lax.ppermute(array, "col", pairs)


def reshuffle(payload):
    devices = lax.axis_size("row") * lax.axis_size("col")
    direct = payload.reshape(devices, NODES // devices, WIDTH)
    moved = lax.all_to_all(direct, ("row", "col"), split_axis=0, concat_axis=0, tiled=True)
    return moved.reshape(payload.shape)


def exchange_planes(payload):
    rows, columns = lax.axis_size("row"), lax.axis_size("col")
    groups = [
        [z * columns + (x * SIDE + y) * CORES + c for z in range(rows) for x in range(SIDE) for c in range(CORES)]
        for y in range(SIDE)
    ]
    direct = payload.reshape(len(groups[0]), NODES // len(groups[0]), WIDTH)
    moved = lax.all_to_all(
        direct, ("row", "col"), split_axis=0, concat_axis=0, tiled=True, axis_index_groups=groups
    )
    return moved.reshape(payload.shape)


def ordering(key_row, key_col):
    below = (key_col[...] < key_row[...]).astype(jnp.int32)
    rank = jnp.sum(below, axis=0, keepdims=True)
    spot = lax.broadcasted_iota(jnp.int32, (NODES, NODES), 0)
    return (spot == rank).astype(F32).astype(BF16)


def order_kernel(key_row, key_col, data, out):
    select = ordering(key_row, key_col)
    out[...] = jnp.dot(select, data[...], preferred_element_type=F32).astype(BF16)


def order_turned_kernel(key_row, key_col, data, out):
    select = ordering(key_row, key_col)
    total = jnp.zeros((NODES, WIDTH), F32)
    for b in range(BLOCKS):
        part = select[:, b * TILE : (b + 1) * TILE]
        block = data[b * WIDTH : (b + 1) * WIDTH, :]
        total += lax.dot_general(part, block, (((1,), (1,)), ((), ())), preferred_element_type=F32)
    out[...] = total.astype(BF16)


def restore_kernel(key_row, key_col, data, out):
    below = (key_row[...] < key_col[...]).astype(jnp.int32)
    rank = jnp.sum(below, axis=1, keepdims=True)
    spot = lax.broadcasted_iota(jnp.int32, (NODES, NODES), 1)
    select = (spot == rank).astype(F32).astype(BF16)
    out[...] = jnp.dot(select, data[...], preferred_element_type=F32).astype(BF16)


def ship_kernel(key_row, key_col, data, turned, *outs):
    select = ordering(key_row, key_col)
    ordered = jnp.dot(select, data[...], preferred_element_type=F32).astype(BF16)
    for k in range(SIDE):
        outs[k][:TURNED, :] = turned[...]
        for h in range(WIDTH // TILE):
            rows = slice(TURNED + h * PART, TURNED + (h + 1) * PART)
            outs[k][rows, :] = ordered[k * PART : (k + 1) * PART, h * TILE : (h + 1) * TILE]


def ship(key, data, turned):
    return pl.pallas_call(
        ship_kernel,
        out_shape=[struct((SHIPPED, TILE), BF16)] * SIDE,
        in_specs=[WHOLE] * 4,
        out_specs=[WHOLE] * SIDE,
        compiler_params=params(),
        cost_estimate=cost(2 * NODES * NODES * WIDTH, 8 * NODES * WIDTH),
    )(key.reshape(1, NODES), key.reshape(NODES, 1), data, turned)


def regroup_kernel(pair, *refs):
    shipped, out = refs[:SIDE], refs[SIDE]
    place = lax.broadcasted_iota(jnp.int32, (NODES, NODES), 0)
    held = lax.broadcasted_iota(jnp.int32, (NODES, NODES), 1)
    peer, step, row = (held % PART) // pair, held // PART, held % pair
    select = (place == (peer * SIDE + step) * pair + row).astype(F32).astype(BF16)
    for h in range(WIDTH // TILE):
        rows = slice(TURNED + h * PART, TURNED + (h + 1) * PART)
        data = jnp.concatenate([part[rows, :] for part in shipped], axis=0)
        total = jnp.dot(select, data, preferred_element_type=F32)
        out[:, h * TILE : (h + 1) * TILE] = total.astype(BF16)


def regroup(shipped, devices):
    return pl.pallas_call(
        functools.partial(regroup_kernel, NODES // devices),
        out_shape=struct((NODES, WIDTH), BF16),
        in_specs=[WHOLE] * SIDE,
        out_specs=WHOLE,
        compiler_params=params(),
        cost_estimate=cost(2 * NODES * NODES * WIDTH, 4 * NODES * WIDTH),
    )(*shipped)


def permute_call(kernel, key, data):
    return pl.pallas_call(
        kernel,
        out_shape=struct((NODES, WIDTH), BF16),
        in_specs=[WHOLE] * 3,
        out_specs=WHOLE,
        compiler_params=params(),
        cost_estimate=cost(2 * NODES * NODES * WIDTH, 4 * NODES * WIDTH),
    )(key.reshape(1, NODES), key.reshape(NODES, 1), data)


def bucket_kernel(target, code, source, *refs):
    outs, (tiles, packed, listed, counts, sent) = refs[:SIDE], refs[SIDE:]
    fetched = pltpu.make_async_copy(source, tiles, sent.at[SIDE])
    fetched.start()
    for d in range(SIDE + 1):
        counts[d] = 0

    def note(s, carry):
        d = target[s]
        n = counts[d]
        listed[d * SLOTS + n] = s
        counts[d] = n + 1
        return carry

    lax.fori_loop(0, SLOTS, note, 0)
    fetched.wait()
    lane = lax.broadcasted_iota(jnp.int32, (CODE_ROWS, TILE), 1)
    copies = []
    for d in (1, 3, 2, 0):
        used = counts[d]

        def place(n, codes, d=d):
            s = listed[d * SLOTS + n]
            packed[d, pl.ds(pl.multiple_of(n * TILE, TILE), TILE), :] = tiles[s]
            return jnp.where(lane == n, code[s], codes)

        def clear(n, carry, d=d):
            rows = pl.ds(pl.multiple_of(n * TILE, TILE), TILE)
            packed[d, rows, :] = jnp.zeros((TILE, TILE), BF16)
            return carry

        codes = lax.fori_loop(0, used, place, jnp.zeros((CODE_ROWS, TILE), jnp.int32))
        lax.fori_loop(used, CAP, clear, 0)
        codes = jnp.where(lane == COUNT_LANE, used, codes)
        packed[d, CAP * TILE :, :] = codes.astype(F32).astype(BF16)
        copies.append(pltpu.make_async_copy(packed.at[d], outs[d], sent.at[d]))
        copies[-1].start()
    for copy in copies:
        copy.wait()


def bucket(tiles, target, code):
    return pl.pallas_call(
        bucket_kernel,
        out_shape=[struct((PACKED, TILE), BF16)] * SIDE,
        in_specs=[SCALARS, SCALARS, FAR],
        out_specs=[FAR] * SIDE,
        scratch_shapes=[
            pltpu.VMEM((SLOTS, TILE, TILE), BF16),
            pltpu.VMEM((SIDE, PACKED, TILE), BF16),
            pltpu.SMEM(((SIDE + 1) * SLOTS,), jnp.int32),
            pltpu.SMEM((SIDE + 1,), jnp.int32),
            pltpu.SemaphoreType.DMA((SIDE + 1,)),
        ],
        compiler_params=params(VMEM_MOST),
        cost_estimate=cost(1e6, 7e6),
    )(target, code, tiles)


def slot_steps(codes):
    most = codes[COUNT_LANE]
    for k in range(1, SIDE):
        most = jnp.maximum(most, codes[k * TILE + COUNT_LANE])
    return (most + 1) // 2


def fetch(sources, places, arrived):
    copies = [
        pltpu.make_async_copy(source, place, arrived.at[i])
        for i, (source, place) in enumerate(zip(sources, places, strict=True))
    ]
    for copy in copies:
        copy.start()
    return copies


def forward_kernel(codes, *refs):
    packs, refs = refs[:SIDE], refs[SIDE:]
    shards, refs = refs[: CORES * SIDE], refs[CORES * SIDE :]
    outs, (tiles, features, arrived, *totals) = refs[:SIDE], refs[SIDE:]
    places = [tiles.at[k] for k in range(SIDE)]
    places += [features.at[pl.ds(j * NODES, NODES)] for j in range(CORES * SIDE)]
    copies = fetch([*packs, *shards], places, arrived)
    for k in range(SIDE):
        totals[k][...] = jnp.zeros((NODES, WIDTH), F32)
    for copy in copies:
        copy.wait()

    def step(i, carry):
        for u in range(2):
            n = i * 2 + u
            for k in range(SIDE):
                code = codes[k * TILE + n]
                row = pl.multiple_of((code // COLUMNS) * TILE, TILE)
                column = pl.multiple_of((code % COLUMNS) * TILE, TILE)
                tile = tiles[k, pl.ds(pl.multiple_of(n * TILE, TILE), TILE), :]
                block = features[pl.ds(column, TILE), :]
                totals[k][pl.ds(row, TILE), :] += jnp.dot(tile, block, preferred_element_type=F32)
        return carry

    lax.fori_loop(0, slot_steps(codes), step, 0)
    for k in range(SIDE):
        outs[k][...] = totals[k][...].astype(outs[k].dtype)


def forward_product(packs, codes, shards):
    shape = (NODES, WIDTH)
    inputs = SIDE + CORES * SIDE
    return pl.pallas_call(
        forward_kernel,
        out_shape=[struct(shape, dtype) for dtype in (F32, BF16, BF16, F32)],
        in_specs=[SCALARS] + [FAR] * inputs,
        out_specs=[WHOLE] * SIDE,
        scratch_shapes=[
            pltpu.VMEM((SIDE, PACKED, TILE), BF16),
            pltpu.VMEM((CORES * SIDE * NODES, WIDTH), BF16),
            pltpu.SemaphoreType.DMA((inputs,)),
        ]
        + [pltpu.VMEM(shape, F32)] * SIDE,
        compiler_params=params(),
        cost_estimate=cost(6e9, 1e6),
    )(codes, *packs, *shards)


def backward_kernel(codes, *refs):
    packs, refs = refs[:SIDE], refs[SIDE:]
    shards, refs = refs[:SIDE], refs[SIDE:]
    near, far, tiles, turned, arrived, totals = refs
    places = [tiles.at[k] for k in range(SIDE)] + [turned.at[k] for k in range(SIDE)]
    shards = [shard.at[pl.ds(0, TURNED)] for shard in shards]
    copies = fetch([*packs, *shards], places, arrived)
    totals[...] = jnp.zeros(totals.shape, F32)
    for copy in copies:
        copy.wait()

    def step(i, carry):
        for u in range(2):
            n = i * 2 + u
            for k in range(SIDE):
                code = codes[k * TILE + n]
                row = pl.multiple_of((code // COLUMNS) * WIDTH, WIDTH)
                column = pl.multiple_of((code % COLUMNS) * WIDTH, WIDTH)
                tile = tiles[k, pl.ds(pl.multiple_of(n * TILE, TILE), TILE), :]
                block = turned[k, pl.ds(row, WIDTH), :]
                totals[pl.ds(column, WIDTH), :] += jnp.dot(block, tile, preferred_element_type=F32)
        return carry

    lax.fori_loop(0, slot_steps(codes), step, 0)
    near[...] = totals[: SIDE * TURNED, :]
    far[...] = totals[SIDE * TURNED :, :].astype(BF16)


def backward_product(packs, codes, shards):
    shape = (SIDE * TURNED, TILE)
    return pl.pallas_call(
        backward_kernel,
        out_shape=[struct(shape, F32), struct(shape, BF16)],
        in_specs=[SCALARS] + [FAR] * (2 * SIDE),
        out_specs=[WHOLE] * CORES,
        scratch_shapes=[
            pltpu.VMEM((SIDE, PACKED, TILE), BF16),
            pltpu.VMEM((SIDE, TURNED, TILE), BF16),
            pltpu.SemaphoreType.DMA((2 * SIDE,)),
            pltpu.VMEM((CORES * SIDE * TURNED, TILE), F32),
        ],
        compiler_params=params(),
        cost_estimate=cost(6e9, 1e6),
    )(codes, *packs, *shards)


ORDER = (2, 1, 3)


def gather_line(array, axis):
    got = {d: move(array, axis, d) for d in ORDER}
    return [array] + [got[d] for d in range(1, SIDE)]


def gather_forward(features):
    one, three = move(features, "x", 1), move(features, "x", -1)
    line = [features, one, move(one, "x", 1), three]
    return line, line + [move(shard, "c", 1) for shard in line]


def scatter_forward(rows):
    passed, back = move(rows[2], "y", 1), move(rows[1], "y", -1)
    ahead = move((rows[3] + passed.astype(F32)).astype(BF16), "y", 1)
    return rows[0] + back.astype(F32) + ahead.astype(F32), back


def add_cores(near, far):
    parts = [slice(j * TURNED, (j + 1) * TURNED) for j in range(SIDE)]
    return [near[part] + far[part].astype(F32) for part in parts]


def add_up(own, arrived):
    for term in arrived:
        own = own + term.astype(F32)
    return own


def after(arrays, others):
    return lax.optimization_barrier((arrays, others))[0]


def shards(
    embeddings,
    partition_source,
    hash_target,
    tile_values,
    tile_row,
    tile_owner,
    tile_sub,
    tile_count,
    cotangent,
):
    index = lax.axis_index("col")
    core = index % CORES
    own_y = (index // CORES) % SIDE
    own_x = index // (CORES * SIDE)

    owner = tile_owner[:, 0]
    live = jnp.arange(SLOTS, dtype=jnp.int32) < tile_count[0]
    back_x = ((own_x - owner // (CORES * SIDE)) * (1 - 2 * (owner % CORES))) % SIDE
    far_y = ((owner // CORES - own_y) * (1 - 2 * core)) % SIDE
    side = (owner + core) % CORES
    column = (side * SIDE + back_x) * BLOCKS + tile_sub
    target = jnp.where(live, far_y, SIDE)
    devices = lax.axis_size("row") * lax.axis_size("col")
    turn = 1 - 2 * core

    def by_plane(device):
        return device // (CORES * SIDE) * CORES + device % CORES, device // CORES % SIDE

    plane, line_y = by_plane(hash_target // NODES)
    key = ((line_y - own_y) * turn) % SIDE * (devices // SIDE) + plane
    turned = cotangent.reshape(BLOCKS, TILE, WIDTH).transpose(0, 2, 1).reshape(TURNED, TILE)
    shipped = ship(key * NODES + hash_target % NODES, embeddings, turned)
    packs = bucket(tile_values, after(target, shipped[0]), tile_row * COLUMNS + column)
    shipped = [shipped[0]] + [move(shipped[k], "y", k) for k in range(1, SIDE)]
    moved = {d: move(after(packs[d], shipped[1]), "y", d) for d in (1, 3)}
    moved[2] = move(after(packs[2], shipped), "y", 2)

    incoming = exchange_planes(regroup(shipped, devices))
    plane, line_y = by_plane(partition_source // NODES)
    turn = 1 - 2 * (plane % CORES)
    key = plane * SIDE + ((own_y - line_y) * turn) % SIDE
    place = jnp.arange(NODES, dtype=jnp.int32)
    initial = permute_call(restore_kernel, key * NODES + place, incoming)
    part_key = (partition_source // NODES) * NODES + place
    packs = [packs[0]] + [moved[d] for d in range(1, SIDE)]
    codes = jnp.concatenate([pack[CAP * TILE] for pack in packs]).astype(jnp.int32)
    line, features = gather_forward(initial)

    def both_products(features, gradients, beside):
        near, far = backward_product(packs, codes, gradients)
        far = move(far, "c", 1)
        if beside:
            rows = forward_product(packs, codes, after(features, near))
            near = after(near, rows[0])
        columns = add_cores(near, far)
        got = {j: move(columns[j].astype(BF16), "x", -j) for j in ORDER}
        if beside:
            rows = after(rows, columns)
        else:
            rows = forward_product(packs, codes, after(features, columns))
            columns[0] = after(columns[0], rows[0])
        total, arrived = scatter_forward(rows)
        if beside:
            columns[0] = after(columns[0], arrived)
        return total, add_up(columns[0], got.values())

    packs = after(packs, line)
    layer_one, back_one = both_products(features, shipped, True)
    layer_one = layer_one.astype(BF16)
    middle = ((turned.astype(F32) + back_one) / 3.0).astype(BF16)
    gradients = gather_line(middle, "y")
    line, features = gather_forward(after(layer_one, middle))
    layer_two, back_zero = both_products(features, after(gradients, line), False)
    grad_part = (turned.astype(F32) / 3.0 + back_zero).astype(BF16)
    returned = reshuffle(permute_call(order_turned_kernel, part_key, grad_part))
    embed_grad = permute_call(restore_kernel, hash_target, returned)
    propagated = ((initial.astype(F32) + layer_one.astype(F32) + layer_two) / 3.0).astype(BF16)
    return propagated, embed_grad


def solution(mesh):
    both = ("row", "col")
    return jax.shard_map(
        shards,
        mesh=mesh,
        in_specs=(
            P(both, None),
            P(both),
            P(both),
            P(both, None, None),
            P(both),
            P(both, None),
            P(both),
            P(both),
            P(both, None),
        ),
        out_specs=(P(both, None), P(both, None)),
        check_vma=False,
    )
```

```python
import functools

import jax
import jax.numpy as jnp
from jax import lax
from jax.experimental import pallas as pl
from jax.experimental.pallas import tpu as pltpu
from jax.sharding import PartitionSpec as P

SIDE = 4
CORES = 2
TILE = 128
NODES = 512
BLOCKS = NODES // TILE
WIDTH = 256
SLOTS = 96
OWNER_CAP = 4
CAP = SIDE * CORES * OWNER_CAP
CODE_ROWS = 16
COUNT_LANE = 64
UNROLL = 8
CHUNK = 8
PACKED = CAP * TILE + CODE_ROWS
COLUMNS = CORES * SIDE * BLOCKS
TURNED = BLOCKS * WIDTH
PART = NODES // SIDE
SHIPPED = TURNED + PART * WIDTH // TILE
BF16 = jnp.bfloat16
F32 = jnp.float32
VMEM_LIMIT = 16 * 1024 * 1024
VMEM_MOST = 62 * 1024 * 1024

WHOLE = pl.BlockSpec(memory_space=pltpu.VMEM)
FAR = pl.BlockSpec(memory_space=pltpu.HBM)
ANY = pl.BlockSpec(memory_space=pl.ANY)
SCALARS = pl.BlockSpec(memory_space=pltpu.SMEM)


def params(limit=VMEM_LIMIT):
    return pltpu.CompilerParams(vmem_limit_bytes=limit)


def struct(shape, dtype):
    return jax.ShapeDtypeStruct(shape, dtype)


def cost(flops, nbytes):
    return pl.CostEstimate(flops=int(flops), bytes_accessed=int(nbytes), transcendentals=0)


def move(array, axis, step):
    pairs = []
    for x in range(SIDE):
        for y in range(SIDE):
            for c in range(CORES):
                ahead = step * (1 - 2 * c)
                to_x = (x + ahead) % SIDE if axis == "x" else x
                to_y = (y + ahead) % SIDE if axis == "y" else y
                to_c = (c + step) % CORES if axis == "c" else c
                pairs.append(((x * SIDE + y) * CORES + c, (to_x * SIDE + to_y) * CORES + to_c))
    return lax.ppermute(array, "col", pairs)


def reshuffle(payload):
    devices = lax.axis_size("row") * lax.axis_size("col")
    direct = payload.reshape(devices, NODES // devices, WIDTH)
    moved = lax.all_to_all(direct, ("row", "col"), split_axis=0, concat_axis=0, tiled=True)
    return moved.reshape(payload.shape)


def exchange_planes(payload):
    rows, columns = lax.axis_size("row"), lax.axis_size("col")
    groups = [
        [z * columns + (x * SIDE + y) * CORES + c for z in range(rows) for x in range(SIDE) for c in range(CORES)]
        for y in range(SIDE)
    ]
    direct = payload.reshape(len(groups[0]), NODES // len(groups[0]), WIDTH)
    moved = lax.all_to_all(
        direct, ("row", "col"), split_axis=0, concat_axis=0, tiled=True, axis_index_groups=groups
    )
    return moved.reshape(payload.shape)


def ordering(key_row, key_col):
    below = (key_col[...] < key_row[...]).astype(jnp.int32)
    rank = jnp.sum(below, axis=0, keepdims=True)
    spot = lax.broadcasted_iota(jnp.int32, (NODES, NODES), 0)
    return (spot == rank).astype(F32).astype(BF16)


def order_kernel(key_row, key_col, data, out):
    select = ordering(key_row, key_col)
    out[...] = jnp.dot(select, data[...], preferred_element_type=F32).astype(BF16)


def order_turned_kernel(key_row, key_col, data, out):
    select = ordering(key_row, key_col)
    total = jnp.zeros((NODES, WIDTH), F32)
    for b in range(BLOCKS):
        part = select[:, b * TILE : (b + 1) * TILE]
        block = data[b * WIDTH : (b + 1) * WIDTH, :]
        total += lax.dot_general(part, block, (((1,), (1,)), ((), ())), preferred_element_type=F32)
    out[...] = total.astype(BF16)


def restore_kernel(key_row, key_col, data, out):
    below = (key_row[...] < key_col[...]).astype(jnp.int32)
    rank = jnp.sum(below, axis=1, keepdims=True)
    spot = lax.broadcasted_iota(jnp.int32, (NODES, NODES), 1)
    select = (spot == rank).astype(F32).astype(BF16)
    out[...] = jnp.dot(select, data[...], preferred_element_type=F32).astype(BF16)


def ship_kernel(key_row, key_col, data, turned, *outs):
    select = ordering(key_row, key_col)
    ordered = jnp.dot(select, data[...], preferred_element_type=F32).astype(BF16)
    for k in range(SIDE):
        outs[k][:TURNED, :] = turned[...]
        for h in range(WIDTH // TILE):
            rows = slice(TURNED + h * PART, TURNED + (h + 1) * PART)
            outs[k][rows, :] = ordered[k * PART : (k + 1) * PART, h * TILE : (h + 1) * TILE]


def ship(key, data, turned):
    return pl.pallas_call(
        ship_kernel,
        out_shape=[struct((SHIPPED, TILE), BF16)] * SIDE,
        in_specs=[WHOLE] * 4,
        out_specs=[WHOLE] * SIDE,
        compiler_params=params(),
        cost_estimate=cost(2 * NODES * NODES * WIDTH, 8 * NODES * WIDTH),
    )(key.reshape(1, NODES), key.reshape(NODES, 1), data, turned)


def regroup_kernel(pair, *refs):
    shipped, out = refs[:SIDE], refs[SIDE]
    place = lax.broadcasted_iota(jnp.int32, (NODES, NODES), 0)
    held = lax.broadcasted_iota(jnp.int32, (NODES, NODES), 1)
    peer, step, row = (held % PART) // pair, held // PART, held % pair
    select = (place == (peer * SIDE + step) * pair + row).astype(F32).astype(BF16)
    for h in range(WIDTH // TILE):
        rows = slice(TURNED + h * PART, TURNED + (h + 1) * PART)
        data = jnp.concatenate([part[rows, :] for part in shipped], axis=0)
        total = jnp.dot(select, data, preferred_element_type=F32)
        out[:, h * TILE : (h + 1) * TILE] = total.astype(BF16)


def regroup(shipped, devices):
    return pl.pallas_call(
        functools.partial(regroup_kernel, NODES // devices),
        out_shape=struct((NODES, WIDTH), BF16),
        in_specs=[WHOLE] * SIDE,
        out_specs=WHOLE,
        compiler_params=params(),
        cost_estimate=cost(2 * NODES * NODES * WIDTH, 4 * NODES * WIDTH),
    )(*shipped)


def permute_call(kernel, key, data):
    return pl.pallas_call(
        kernel,
        out_shape=struct((NODES, WIDTH), BF16),
        in_specs=[WHOLE] * 3,
        out_specs=WHOLE,
        compiler_params=params(),
        cost_estimate=cost(2 * NODES * NODES * WIDTH, 4 * NODES * WIDTH),
    )(key.reshape(1, NODES), key.reshape(NODES, 1), data)


def bucket_kernel(target, code, source, *refs):
    outs, (tiles, packed, listed, counts, sent) = refs[:SIDE], refs[SIDE:]
    fetched = pltpu.make_async_copy(source, tiles, sent.at[SIDE])
    fetched.start()
    for d in range(SIDE + 1):
        counts[d] = 0

    def note(s, carry):
        d = target[s]
        n = counts[d]
        listed[d * SLOTS + n] = s
        counts[d] = n + 1
        return carry

    lax.fori_loop(0, SLOTS, note, 0)
    fetched.wait()
    lane = lax.broadcasted_iota(jnp.int32, (CODE_ROWS, TILE), 1)
    copies = []
    for d in (1, 3, 2, 0):
        used = counts[d]

        def place(n, codes, d=d):
            s = listed[d * SLOTS + n]
            packed[d, pl.ds(pl.multiple_of(n * TILE, TILE), TILE), :] = tiles[s]
            return jnp.where(lane == n, code[s], codes)

        def clear(n, carry, d=d):
            rows = pl.ds(pl.multiple_of(n * TILE, TILE), TILE)
            packed[d, rows, :] = jnp.zeros((TILE, TILE), BF16)
            return carry

        codes = lax.fori_loop(0, used, place, jnp.zeros((CODE_ROWS, TILE), jnp.int32))
        lax.fori_loop(used, CAP, clear, 0)
        codes = jnp.where(lane == COUNT_LANE, used, codes)
        packed[d, CAP * TILE :, :] = codes.astype(F32).astype(BF16)
        copies.append(pltpu.make_async_copy(packed.at[d], outs[d], sent.at[d]))
        copies[-1].start()
    for copy in copies:
        copy.wait()


def bucket(tiles, target, code):
    return pl.pallas_call(
        bucket_kernel,
        out_shape=[struct((PACKED, TILE), BF16)] * SIDE,
        in_specs=[SCALARS, SCALARS, FAR],
        out_specs=[FAR] * SIDE,
        scratch_shapes=[
            pltpu.VMEM((SLOTS, TILE, TILE), BF16),
            pltpu.VMEM((SIDE, PACKED, TILE), BF16),
            pltpu.SMEM(((SIDE + 1) * SLOTS,), jnp.int32),
            pltpu.SMEM((SIDE + 1,), jnp.int32),
            pltpu.SemaphoreType.DMA((SIDE + 1,)),
        ],
        compiler_params=params(VMEM_MOST),
        cost_estimate=cost(1e6, 7e6),
    )(target, code, tiles)


def fetch_packs(codes, packs, tiles, arrived):
    rows = CHUNK * TILE
    waits = []
    for k in range(SIDE):
        for i in range(CAP // CHUNK):
            source = packs[k].at[pl.ds(i * rows, rows)]
            place = tiles.at[pl.ds(k * CAP * TILE + i * rows, rows)]
            copy = pltpu.make_async_copy(source, place, arrived.at[k * (CAP // CHUNK) + i])
            used = codes[k * TILE + COUNT_LANE] > i * CHUNK
            pl.when(used)(copy.start)
            waits.append((used, copy))

    def wait():
        for used, copy in waits:
            pl.when(used)(copy.wait)

    return wait


def list_slots(codes, slots):
    total = jnp.int32(0)
    for k in range(SIDE):

        def note(n, at, k=k):
            code = codes[k * TILE + n]
            slots[0, at] = k * CAP + n
            slots[1, at] = k * BLOCKS + code // COLUMNS
            slots[2, at] = code % COLUMNS
            return at + 1

        total = lax.fori_loop(0, codes[k * TILE + COUNT_LANE], note, total)
    for u in range(UNROLL):
        slots[0, total + u] = SIDE * CAP
        slots[1, total + u] = 0
        slots[2, total + u] = 0
    return (total + UNROLL - 1) // UNROLL


def slot_block(slots, i, at, size):
    return pl.ds(pl.multiple_of(slots[i, at] * size, size), size)


def fetch(sources, places, arrived):
    copies = [
        pltpu.make_async_copy(source, place, arrived.at[i])
        for i, (source, place) in enumerate(zip(sources, places, strict=True))
    ]
    for copy in copies:
        copy.start()
    return copies


def forward_kernel(codes, *refs):
    packs, refs = refs[:SIDE], refs[SIDE:]
    shards, refs = refs[: CORES * SIDE], refs[CORES * SIDE :]
    outs, (tiles, features, totals, slots, arrived, fetched) = refs[:SIDE], refs[SIDE:]
    places = [features.at[pl.ds(j * NODES, NODES)] for j in range(CORES * SIDE)]
    wait = fetch_packs(codes, packs, tiles, fetched)
    copies = fetch(shards, places, arrived)
    totals[...] = jnp.zeros(totals.shape, F32)
    tiles[SIDE * CAP * TILE :, :] = jnp.zeros((TILE, TILE), BF16)
    steps = list_slots(codes, slots)
    for copy in copies:
        copy.wait()
    wait()

    def step(i, carry):
        for u in range(UNROLL):
            at = i * UNROLL + u
            tile = tiles[slot_block(slots, 0, at, TILE), :]
            block = features[slot_block(slots, 2, at, TILE), :]
            to = slot_block(slots, 1, at, TILE)
            totals[to, :] += jnp.dot(tile, block, preferred_element_type=F32)
        return carry

    lax.fori_loop(0, steps, step, 0)
    for k in range(SIDE):
        outs[k][...] = totals[k * NODES : (k + 1) * NODES, :].astype(outs[k].dtype)


def forward_product(packs, codes, shards):
    shape = (NODES, WIDTH)
    inputs = SIDE + CORES * SIDE
    return pl.pallas_call(
        forward_kernel,
        out_shape=[struct(shape, dtype) for dtype in (F32, BF16, BF16, F32)],
        in_specs=[SCALARS] + [ANY] * inputs,
        out_specs=[WHOLE] * SIDE,
        scratch_shapes=[
            pltpu.VMEM(((SIDE * CAP + 1) * TILE, TILE), BF16),
            pltpu.VMEM((CORES * SIDE * NODES, WIDTH), BF16),
            pltpu.VMEM((SIDE * NODES, WIDTH), F32),
            pltpu.SMEM((3, SIDE * CAP + UNROLL), jnp.int32),
            pltpu.SemaphoreType.DMA((CORES * SIDE,)),
            pltpu.SemaphoreType.DMA((SIDE * CAP // CHUNK,)),
        ],
        compiler_params=params(),
        cost_estimate=cost(6e9, 1e6),
    )(codes, *packs, *shards)


def backward_kernel(codes, *refs):
    packs, refs = refs[:SIDE], refs[SIDE:]
    shards, refs = refs[:SIDE], refs[SIDE:]
    near, refs = refs[:SIDE], refs[SIDE:]
    far, tiles, turned, totals, slots, arrived, fetched = refs
    places = [turned.at[pl.ds(k * TURNED, TURNED)] for k in range(SIDE)]
    wait = fetch_packs(codes, packs, tiles, fetched)
    copies = fetch([shard.at[pl.ds(0, TURNED)] for shard in shards], places, arrived)
    totals[...] = jnp.zeros(totals.shape, F32)
    tiles[SIDE * CAP * TILE :, :] = jnp.zeros((TILE, TILE), BF16)
    steps = list_slots(codes, slots)
    for copy in copies:
        copy.wait()
    wait()

    def step(i, carry):
        for u in range(UNROLL):
            at = i * UNROLL + u
            tile = tiles[slot_block(slots, 0, at, TILE), :]
            block = turned[slot_block(slots, 1, at, WIDTH), :]
            to = slot_block(slots, 2, at, WIDTH)
            totals[to, :] += jnp.dot(block, tile, preferred_element_type=F32)
        return carry

    lax.fori_loop(0, steps, step, 0)
    for j in range(SIDE):
        near[j][...] = totals[j * TURNED : (j + 1) * TURNED, :]
    far[...] = totals[SIDE * TURNED :, :].astype(BF16)


def backward_product(packs, codes, shards):
    *near, far = pl.pallas_call(
        backward_kernel,
        out_shape=[struct((TURNED, TILE), F32)] * SIDE + [struct((SIDE * TURNED, TILE), BF16)],
        in_specs=[SCALARS] + [ANY] * (2 * SIDE),
        out_specs=[WHOLE] * (SIDE + 1),
        scratch_shapes=[
            pltpu.VMEM(((SIDE * CAP + 1) * TILE, TILE), BF16),
            pltpu.VMEM((SIDE * TURNED, TILE), BF16),
            pltpu.VMEM((CORES * SIDE * TURNED, TILE), F32),
            pltpu.SMEM((3, SIDE * CAP + UNROLL), jnp.int32),
            pltpu.SemaphoreType.DMA((SIDE,)),
            pltpu.SemaphoreType.DMA((SIDE * CAP // CHUNK,)),
        ],
        compiler_params=params(),
        cost_estimate=cost(6e9, 1e6),
    )(codes, *packs, *shards)
    return near, far


ORDER = (2, 1, 3)


def gather_line(array, axis):
    got = {d: move(array, axis, d) for d in ORDER}
    return [array] + [got[d] for d in range(1, SIDE)]


def gather_forward(features):
    one, three = move(features, "x", 1), move(features, "x", -1)
    line = [features, one, move(one, "x", 1), three]
    return line, line + [move(shard, "c", 1) for shard in line]


def scatter_forward(rows):
    passed, back = move(rows[2], "y", 1), move(rows[1], "y", -1)
    ahead = move((rows[3] + passed.astype(F32)).astype(BF16), "y", 1)
    return rows[0] + back.astype(F32) + ahead.astype(F32), back


def add_cores(near, far):
    parts = [slice(j * TURNED, (j + 1) * TURNED) for j in range(SIDE)]
    return [own + far[part].astype(F32) for own, part in zip(near, parts, strict=True)]


def add_up(own, arrived):
    for term in arrived:
        own = own + term.astype(F32)
    return own


def after(arrays, others):
    return lax.optimization_barrier((arrays, others))[0]


def shards(
    embeddings,
    partition_source,
    hash_target,
    tile_values,
    tile_row,
    tile_owner,
    tile_sub,
    tile_count,
    cotangent,
):
    index = lax.axis_index("col")
    core = index % CORES
    own_y = (index // CORES) % SIDE
    own_x = index // (CORES * SIDE)

    owner = tile_owner[:, 0]
    live = jnp.arange(SLOTS, dtype=jnp.int32) < tile_count[0]
    back_x = ((own_x - owner // (CORES * SIDE)) * (1 - 2 * (owner % CORES))) % SIDE
    far_y = ((owner // CORES - own_y) * (1 - 2 * core)) % SIDE
    side = (owner + core) % CORES
    column = (side * SIDE + back_x) * BLOCKS + tile_sub
    target = jnp.where(live, far_y, SIDE)
    devices = lax.axis_size("row") * lax.axis_size("col")
    turn = 1 - 2 * core

    def by_plane(device):
        return device // (CORES * SIDE) * CORES + device % CORES, device // CORES % SIDE

    plane, line_y = by_plane(hash_target // NODES)
    key = ((line_y - own_y) * turn) % SIDE * (devices // SIDE) + plane
    turned = cotangent.reshape(BLOCKS, TILE, WIDTH).transpose(0, 2, 1).reshape(TURNED, TILE)
    shipped = ship(key * NODES + hash_target % NODES, embeddings, turned)
    packs = bucket(tile_values, after(target, shipped[0]), tile_row * COLUMNS + column)
    shipped = [shipped[0]] + [move(shipped[k], "y", k) for k in range(1, SIDE)]
    moved = {d: move(after(packs[d], shipped[1]), "y", d) for d in (1, 3)}
    moved[2] = move(after(packs[2], shipped), "y", 2)

    incoming = exchange_planes(regroup(shipped, devices))
    plane, line_y = by_plane(partition_source // NODES)
    turn = 1 - 2 * (plane % CORES)
    key = plane * SIDE + ((own_y - line_y) * turn) % SIDE
    place = jnp.arange(NODES, dtype=jnp.int32)
    initial = permute_call(restore_kernel, key * NODES + place, incoming)
    part_key = (partition_source // NODES) * NODES + place
    packs = [packs[0]] + [moved[d] for d in range(1, SIDE)]
    codes = jnp.concatenate([pack[CAP * TILE] for pack in packs]).astype(jnp.int32)
    line, features = gather_forward(initial)

    def both_products(features, gradients, beside):
        near, far = backward_product(packs, codes, gradients)
        far = move(far, "c", 1)
        if beside:
            rows = forward_product(packs, codes, after(features, near))
            near = after(near, rows[0])
        columns = add_cores(near, far)
        got = {j: move(columns[j].astype(BF16), "x", -j) for j in ORDER}
        if beside:
            rows = after(rows, columns)
        else:
            rows = forward_product(packs, codes, after(features, columns))
            columns[0] = after(columns[0], rows[0])
        total, arrived = scatter_forward(rows)
        if beside:
            columns[0] = after(columns[0], arrived)
        return total, add_up(columns[0], got.values())

    packs = after(packs, line)
    layer_one, back_one = both_products(features, shipped, True)
    layer_one = layer_one.astype(BF16)
    middle = ((turned.astype(F32) + back_one) / 3.0).astype(BF16)
    gradients = gather_line(middle, "y")
    line, features = gather_forward(after(layer_one, middle))
    layer_two, back_zero = both_products(features, after(gradients, line), False)
    grad_part = (turned.astype(F32) / 3.0 + back_zero).astype(BF16)
    returned = reshuffle(permute_call(order_turned_kernel, part_key, grad_part))
    embed_grad = permute_call(restore_kernel, hash_target, returned)
    propagated = ((initial.astype(F32) + layer_one.astype(F32) + layer_two) / 3.0).astype(BF16)
    return propagated, embed_grad


def solution(mesh):
    both = ("row", "col")
    return jax.shard_map(
        shards,
        mesh=mesh,
        in_specs=(
            P(both, None),
            P(both),
            P(both),
            P(both, None, None),
            P(both),
            P(both, None),
            P(both),
            P(both),
            P(both, None),
        ),
        out_specs=(P(both, None), P(both, None)),
        check_vma=False,
    )
```

```python
import functools

import jax
import jax.numpy as jnp
from jax import lax
from jax.experimental import pallas as pl
from jax.experimental.pallas import tpu as pltpu
from jax.sharding import PartitionSpec as P

SIDE = 4
CORES = 2
TILE = 128
NODES = 512
BLOCKS = NODES // TILE
WIDTH = 256
SLOTS = 96
OWNER_CAP = 4
CAP = SIDE * CORES * OWNER_CAP
CODE_ROWS = 16
COUNT_LANE = 64
UNROLL = 16
CHUNK = 8
PACKED = CAP * TILE + CODE_ROWS
COLUMNS = CORES * SIDE * BLOCKS
TURNED = BLOCKS * WIDTH
PART = NODES // SIDE
SHIPPED = TURNED + PART * WIDTH // TILE
BF16 = jnp.bfloat16
F32 = jnp.float32
VMEM_LIMIT = 16 * 1024 * 1024
VMEM_MOST = 62 * 1024 * 1024

WHOLE = pl.BlockSpec(memory_space=pltpu.VMEM)
FAR = pl.BlockSpec(memory_space=pltpu.HBM)
ANY = pl.BlockSpec(memory_space=pl.ANY)
SCALARS = pl.BlockSpec(memory_space=pltpu.SMEM)


def params(limit=VMEM_LIMIT):
    return pltpu.CompilerParams(vmem_limit_bytes=limit)


def struct(shape, dtype):
    return jax.ShapeDtypeStruct(shape, dtype)


def cost(flops, nbytes):
    return pl.CostEstimate(flops=int(flops), bytes_accessed=int(nbytes), transcendentals=0)


def move(array, axis, step):
    pairs = []
    for x in range(SIDE):
        for y in range(SIDE):
            for c in range(CORES):
                ahead = step * (1 - 2 * c)
                to_x = (x + ahead) % SIDE if axis == "x" else x
                to_y = (y + ahead) % SIDE if axis == "y" else y
                to_c = (c + step) % CORES if axis == "c" else c
                pairs.append(((x * SIDE + y) * CORES + c, (to_x * SIDE + to_y) * CORES + to_c))
    return lax.ppermute(array, "col", pairs)


def reshuffle(payload):
    devices = lax.axis_size("row") * lax.axis_size("col")
    direct = payload.reshape(devices, NODES // devices, WIDTH)
    moved = lax.all_to_all(direct, ("row", "col"), split_axis=0, concat_axis=0, tiled=True)
    return moved.reshape(payload.shape)


def exchange_planes(payload):
    rows, columns = lax.axis_size("row"), lax.axis_size("col")
    groups = [
        [z * columns + (x * SIDE + y) * CORES + c for z in range(rows) for x in range(SIDE) for c in range(CORES)]
        for y in range(SIDE)
    ]
    direct = payload.reshape(len(groups[0]), NODES // len(groups[0]), WIDTH)
    moved = lax.all_to_all(
        direct, ("row", "col"), split_axis=0, concat_axis=0, tiled=True, axis_index_groups=groups
    )
    return moved.reshape(payload.shape)


def ordering(key_row, key_col):
    below = (key_col[...] < key_row[...]).astype(jnp.int32)
    rank = jnp.sum(below, axis=0, keepdims=True)
    spot = lax.broadcasted_iota(jnp.int32, (NODES, NODES), 0)
    return (spot == rank).astype(F32).astype(BF16)


def order_kernel(key_row, key_col, data, out):
    select = ordering(key_row, key_col)
    out[...] = jnp.dot(select, data[...], preferred_element_type=F32).astype(BF16)


def order_turned_kernel(key_row, key_col, data, out):
    select = ordering(key_row, key_col)
    total = jnp.zeros((NODES, WIDTH), F32)
    for b in range(BLOCKS):
        part = select[:, b * TILE : (b + 1) * TILE]
        block = data[b * WIDTH : (b + 1) * WIDTH, :]
        total += lax.dot_general(part, block, (((1,), (1,)), ((), ())), preferred_element_type=F32)
    out[...] = total.astype(BF16)


def restore_kernel(key_row, key_col, data, out):
    below = (key_row[...] < key_col[...]).astype(jnp.int32)
    rank = jnp.sum(below, axis=1, keepdims=True)
    spot = lax.broadcasted_iota(jnp.int32, (NODES, NODES), 1)
    select = (spot == rank).astype(F32).astype(BF16)
    out[...] = jnp.dot(select, data[...], preferred_element_type=F32).astype(BF16)


def ship_kernel(key_row, key_col, data, turned, *outs):
    select = ordering(key_row, key_col)
    ordered = jnp.dot(select, data[...], preferred_element_type=F32).astype(BF16)
    for k in range(SIDE):
        outs[k][:TURNED, :] = turned[...]
        for h in range(WIDTH // TILE):
            rows = slice(TURNED + h * PART, TURNED + (h + 1) * PART)
            outs[k][rows, :] = ordered[k * PART : (k + 1) * PART, h * TILE : (h + 1) * TILE]


def ship(key, data, turned):
    return pl.pallas_call(
        ship_kernel,
        out_shape=[struct((SHIPPED, TILE), BF16)] * SIDE,
        in_specs=[WHOLE] * 4,
        out_specs=[WHOLE] * SIDE,
        compiler_params=params(),
        cost_estimate=cost(2 * NODES * NODES * WIDTH, 8 * NODES * WIDTH),
    )(key.reshape(1, NODES), key.reshape(NODES, 1), data, turned)


def regroup_kernel(pair, *refs):
    shipped, out = refs[:SIDE], refs[SIDE]
    place = lax.broadcasted_iota(jnp.int32, (NODES, NODES), 0)
    held = lax.broadcasted_iota(jnp.int32, (NODES, NODES), 1)
    peer, step, row = (held % PART) // pair, held // PART, held % pair
    select = (place == (peer * SIDE + step) * pair + row).astype(F32).astype(BF16)
    for h in range(WIDTH // TILE):
        rows = slice(TURNED + h * PART, TURNED + (h + 1) * PART)
        data = jnp.concatenate([part[rows, :] for part in shipped], axis=0)
        total = jnp.dot(select, data, preferred_element_type=F32)
        out[:, h * TILE : (h + 1) * TILE] = total.astype(BF16)


def regroup(shipped, devices):
    return pl.pallas_call(
        functools.partial(regroup_kernel, NODES // devices),
        out_shape=struct((NODES, WIDTH), BF16),
        in_specs=[WHOLE] * SIDE,
        out_specs=WHOLE,
        compiler_params=params(),
        cost_estimate=cost(2 * NODES * NODES * WIDTH, 4 * NODES * WIDTH),
    )(*shipped)


def permute_call(kernel, key, data):
    return pl.pallas_call(
        kernel,
        out_shape=struct((NODES, WIDTH), BF16),
        in_specs=[WHOLE] * 3,
        out_specs=WHOLE,
        compiler_params=params(),
        cost_estimate=cost(2 * NODES * NODES * WIDTH, 4 * NODES * WIDTH),
    )(key.reshape(1, NODES), key.reshape(NODES, 1), data)


def bucket_kernel(target, code, source, *refs):
    outs, (tiles, packed, listed, counts, sent) = refs[:SIDE], refs[SIDE:]
    fetched = pltpu.make_async_copy(source, tiles, sent.at[SIDE])
    fetched.start()
    for d in range(SIDE + 1):
        counts[d] = 0

    def note(s, carry):
        d = target[s]
        n = counts[d]
        listed[d * SLOTS + n] = s
        counts[d] = n + 1
        return carry

    lax.fori_loop(0, SLOTS, note, 0)
    fetched.wait()
    lane = lax.broadcasted_iota(jnp.int32, (CODE_ROWS, TILE), 1)
    copies = []
    for d in (1, 3, 2, 0):
        used = counts[d]

        def place(n, codes, d=d):
            s = listed[d * SLOTS + n]
            packed[d, pl.ds(pl.multiple_of(n * TILE, TILE), TILE), :] = tiles[s]
            return jnp.where(lane == n, code[s], codes)

        def clear(n, carry, d=d):
            rows = pl.ds(pl.multiple_of(n * TILE, TILE), TILE)
            packed[d, rows, :] = jnp.zeros((TILE, TILE), BF16)
            return carry

        codes = lax.fori_loop(0, used, place, jnp.zeros((CODE_ROWS, TILE), jnp.int32))
        lax.fori_loop(used, CAP, clear, 0)
        codes = jnp.where(lane == COUNT_LANE, used, codes)
        packed[d, CAP * TILE :, :] = codes.astype(F32).astype(BF16)
        copies.append(pltpu.make_async_copy(packed.at[d], outs[d], sent.at[d]))
        copies[-1].start()
    for copy in copies:
        copy.wait()


def bucket(tiles, target, code):
    return pl.pallas_call(
        bucket_kernel,
        out_shape=[struct((PACKED, TILE), BF16)] * SIDE,
        in_specs=[SCALARS, SCALARS, FAR],
        out_specs=[FAR] * SIDE,
        scratch_shapes=[
            pltpu.VMEM((SLOTS, TILE, TILE), BF16),
            pltpu.VMEM((SIDE, PACKED, TILE), BF16),
            pltpu.SMEM(((SIDE + 1) * SLOTS,), jnp.int32),
            pltpu.SMEM((SIDE + 1,), jnp.int32),
            pltpu.SemaphoreType.DMA((SIDE + 1,)),
        ],
        compiler_params=params(VMEM_MOST),
        cost_estimate=cost(1e6, 7e6),
    )(target, code, tiles)


def fetch_packs(codes, packs, tiles, arrived):
    rows = CHUNK * TILE
    waits = []
    for k in range(SIDE):
        for i in range(CAP // CHUNK):
            source = packs[k].at[pl.ds(i * rows, rows)]
            place = tiles.at[pl.ds(k * CAP * TILE + i * rows, rows)]
            copy = pltpu.make_async_copy(source, place, arrived.at[k * (CAP // CHUNK) + i])
            used = codes[k * TILE + COUNT_LANE] > i * CHUNK
            pl.when(used)(copy.start)
            waits.append((used, copy))

    def wait():
        for used, copy in waits:
            pl.when(used)(copy.wait)

    return wait


def list_slots(codes, slots):
    total = jnp.int32(0)
    for k in range(SIDE):

        def note(n, at, k=k):
            code = codes[k * TILE + n]
            slots[0, at] = k * CAP + n
            slots[1, at] = k * BLOCKS + code // COLUMNS
            slots[2, at] = code % COLUMNS
            return at + 1

        total = lax.fori_loop(0, codes[k * TILE + COUNT_LANE], note, total)
    for u in range(UNROLL):
        slots[0, total + u] = SIDE * CAP
        slots[1, total + u] = 0
        slots[2, total + u] = 0
    return (total + UNROLL - 1) // UNROLL


def slot_block(slots, i, at, size):
    return pl.ds(pl.multiple_of(slots[i, at] * size, size), size)


def fetch(sources, places, arrived):
    copies = [
        pltpu.make_async_copy(source, place, arrived.at[i])
        for i, (source, place) in enumerate(zip(sources, places, strict=True))
    ]
    for copy in copies:
        copy.start()
    return copies


def forward_kernel(codes, *refs):
    packs, refs = refs[:SIDE], refs[SIDE:]
    shards, refs = refs[: CORES * SIDE], refs[CORES * SIDE :]
    outs, (tiles, features, totals, slots, arrived, fetched) = refs[:SIDE], refs[SIDE:]
    places = [features.at[pl.ds(j * NODES, NODES)] for j in range(CORES * SIDE)]
    wait = fetch_packs(codes, packs, tiles, fetched)
    copies = fetch(shards, places, arrived)
    totals[...] = jnp.zeros(totals.shape, F32)
    tiles[SIDE * CAP * TILE :, :] = jnp.zeros((TILE, TILE), BF16)
    steps = list_slots(codes, slots)
    for copy in copies:
        copy.wait()
    wait()

    def step(i, carry):
        for u in range(UNROLL):
            at = i * UNROLL + u
            tile = tiles[slot_block(slots, 0, at, TILE), :]
            block = features[slot_block(slots, 2, at, TILE), :]
            to = slot_block(slots, 1, at, TILE)
            totals[to, :] += jnp.dot(tile, block, preferred_element_type=F32)
        return carry

    lax.fori_loop(0, steps, step, 0)
    for k in range(SIDE):
        outs[k][...] = totals[k * NODES : (k + 1) * NODES, :].astype(outs[k].dtype)


def forward_product(packs, codes, shards):
    shape = (NODES, WIDTH)
    inputs = SIDE + CORES * SIDE
    return pl.pallas_call(
        forward_kernel,
        out_shape=[struct(shape, dtype) for dtype in (F32, BF16, BF16, F32)],
        in_specs=[SCALARS] + [ANY] * inputs,
        out_specs=[WHOLE] * SIDE,
        scratch_shapes=[
            pltpu.VMEM(((SIDE * CAP + 1) * TILE, TILE), BF16),
            pltpu.VMEM((CORES * SIDE * NODES, WIDTH), BF16),
            pltpu.VMEM((SIDE * NODES, WIDTH), F32),
            pltpu.SMEM((3, SIDE * CAP + UNROLL), jnp.int32),
            pltpu.SemaphoreType.DMA((CORES * SIDE,)),
            pltpu.SemaphoreType.DMA((SIDE * CAP // CHUNK,)),
        ],
        compiler_params=params(),
        cost_estimate=cost(6e9, 1e6),
    )(codes, *packs, *shards)


def backward_kernel(codes, *refs):
    packs, refs = refs[:SIDE], refs[SIDE:]
    shards, refs = refs[:SIDE], refs[SIDE:]
    near, refs = refs[:SIDE], refs[SIDE:]
    far, tiles, turned, totals, slots, arrived, fetched = refs
    places = [turned.at[pl.ds(k * TURNED, TURNED)] for k in range(SIDE)]
    wait = fetch_packs(codes, packs, tiles, fetched)
    copies = fetch([shard.at[pl.ds(0, TURNED)] for shard in shards], places, arrived)
    totals[...] = jnp.zeros(totals.shape, F32)
    tiles[SIDE * CAP * TILE :, :] = jnp.zeros((TILE, TILE), BF16)
    steps = list_slots(codes, slots)
    for copy in copies:
        copy.wait()
    wait()

    def step(i, carry):
        for u in range(UNROLL):
            at = i * UNROLL + u
            tile = tiles[slot_block(slots, 0, at, TILE), :]
            block = turned[slot_block(slots, 1, at, WIDTH), :]
            to = slot_block(slots, 2, at, WIDTH)
            totals[to, :] += jnp.dot(block, tile, preferred_element_type=F32)
        return carry

    lax.fori_loop(0, steps, step, 0)
    for j in range(SIDE):
        near[j][...] = totals[j * TURNED : (j + 1) * TURNED, :].astype(near[j].dtype)
    far[...] = totals[SIDE * TURNED :, :].astype(BF16)


def backward_product(packs, codes, shards):
    *near, far = pl.pallas_call(
        backward_kernel,
        out_shape=[struct((TURNED, TILE), F32)]
        + [struct((TURNED, TILE), BF16)] * (SIDE - 1)
        + [struct((SIDE * TURNED, TILE), BF16)],
        in_specs=[SCALARS] + [ANY] * (2 * SIDE),
        out_specs=[WHOLE] * (SIDE + 1),
        scratch_shapes=[
            pltpu.VMEM(((SIDE * CAP + 1) * TILE, TILE), BF16),
            pltpu.VMEM((SIDE * TURNED, TILE), BF16),
            pltpu.VMEM((CORES * SIDE * TURNED, TILE), F32),
            pltpu.SMEM((3, SIDE * CAP + UNROLL), jnp.int32),
            pltpu.SemaphoreType.DMA((SIDE,)),
            pltpu.SemaphoreType.DMA((SIDE * CAP // CHUNK,)),
        ],
        compiler_params=params(),
        cost_estimate=cost(6e9, 1e6),
    )(codes, *packs, *shards)
    return near, far


ORDER = (2, 1, 3)


def gather_line(array, axis):
    got = {d: move(array, axis, d) for d in ORDER}
    return [array] + [got[d] for d in range(1, SIDE)]


def gather_forward(features):
    one, three = move(features, "x", 1), move(features, "x", -1)
    line = [features, one, move(one, "x", 1), three]
    return line, line + [move(shard, "c", 1) for shard in line]


def scatter_forward(rows):
    passed, back = move(rows[2], "y", 1), move(rows[1], "y", -1)
    ahead = move((rows[3] + passed.astype(F32)).astype(BF16), "y", 1)
    return rows[0] + back.astype(F32) + ahead.astype(F32), back


def add_cores(near, far):
    parts = [slice(j * TURNED, (j + 1) * TURNED) for j in range(SIDE)]
    pairs = zip(near, parts, strict=True)
    return [own.astype(F32) + far[part].astype(F32) for own, part in pairs]


def add_up(own, arrived):
    for term in arrived:
        own = own + term.astype(F32)
    return own


def after(arrays, others):
    return lax.optimization_barrier((arrays, others))[0]


def shards(
    embeddings,
    partition_source,
    hash_target,
    tile_values,
    tile_row,
    tile_owner,
    tile_sub,
    tile_count,
    cotangent,
):
    index = lax.axis_index("col")
    core = index % CORES
    own_y = (index // CORES) % SIDE
    own_x = index // (CORES * SIDE)

    owner = tile_owner[:, 0]
    live = jnp.arange(SLOTS, dtype=jnp.int32) < tile_count[0]
    back_x = ((own_x - owner // (CORES * SIDE)) * (1 - 2 * (owner % CORES))) % SIDE
    far_y = ((owner // CORES - own_y) * (1 - 2 * core)) % SIDE
    side = (owner + core) % CORES
    column = (side * SIDE + back_x) * BLOCKS + tile_sub
    target = jnp.where(live, far_y, SIDE)
    devices = lax.axis_size("row") * lax.axis_size("col")
    turn = 1 - 2 * core

    def by_plane(device):
        return device // (CORES * SIDE) * CORES + device % CORES, device // CORES % SIDE

    plane, line_y = by_plane(hash_target // NODES)
    key = ((line_y - own_y) * turn) % SIDE * (devices // SIDE) + plane
    turned = cotangent.reshape(BLOCKS, TILE, WIDTH).transpose(0, 2, 1).reshape(TURNED, TILE)
    shipped = ship(key * NODES + hash_target % NODES, embeddings, turned)
    packs = bucket(tile_values, after(target, shipped[0]), tile_row * COLUMNS + column)
    shipped = [shipped[0]] + [move(shipped[k], "y", k) for k in range(1, SIDE)]
    moved = {d: move(after(packs[d], shipped[1]), "y", d) for d in (1, 3)}
    moved[2] = move(after(packs[2], shipped), "y", 2)

    incoming = exchange_planes(regroup(shipped, devices))
    plane, line_y = by_plane(partition_source // NODES)
    turn = 1 - 2 * (plane % CORES)
    key = plane * SIDE + ((own_y - line_y) * turn) % SIDE
    place = jnp.arange(NODES, dtype=jnp.int32)
    initial = permute_call(restore_kernel, key * NODES + place, incoming)
    part_key = (partition_source // NODES) * NODES + place
    packs = [packs[0]] + [moved[d] for d in range(1, SIDE)]
    codes = jnp.concatenate([pack[CAP * TILE] for pack in packs]).astype(jnp.int32)
    line, features = gather_forward(initial)

    def both_products(features, gradients, beside):
        near, far = backward_product(packs, codes, gradients)
        far = move(far, "c", 1)
        if beside:
            rows = forward_product(packs, codes, after(features, near))
            near = after(near, rows[0])
        columns = add_cores(near, far)
        got = {j: move(columns[j].astype(BF16), "x", -j) for j in ORDER}
        if beside:
            rows = after(rows, columns)
        else:
            rows = forward_product(packs, codes, after(features, columns))
            columns[0] = after(columns[0], rows[0])
        total, arrived = scatter_forward(rows)
        if beside:
            columns[0] = after(columns[0], arrived)
        return total, add_up(columns[0], got.values())

    packs = after(packs, line)
    layer_one, back_one = both_products(features, shipped, True)
    layer_one = layer_one.astype(BF16)
    middle = ((turned.astype(F32) + back_one) / 3.0).astype(BF16)
    gradients = gather_line(middle, "y")
    line, features = gather_forward(after(layer_one, middle))
    layer_two, back_zero = both_products(features, after(gradients, line), False)
    grad_part = (turned.astype(F32) / 3.0 + back_zero).astype(BF16)
    returned = reshuffle(permute_call(order_turned_kernel, part_key, grad_part))
    embed_grad = permute_call(restore_kernel, hash_target, returned)
    propagated = ((initial.astype(F32) + layer_one.astype(F32) + layer_two) / 3.0).astype(BF16)
    return propagated, embed_grad


def solution(mesh):
    both = ("row", "col")
    return jax.shard_map(
        shards,
        mesh=mesh,
        in_specs=(
            P(both, None),
            P(both),
            P(both),
            P(both, None, None),
            P(both),
            P(both, None),
            P(both),
            P(both),
            P(both, None),
        ),
        out_specs=(P(both, None), P(both, None)),
        check_vma=False,
    )
```

```python
import functools

import jax
import jax.numpy as jnp
from jax import lax
from jax.experimental import pallas as pl
from jax.experimental.pallas import tpu as pltpu
from jax.sharding import PartitionSpec as P

SIDE = 4
CORES = 2
TILE = 128
NODES = 512
BLOCKS = NODES // TILE
WIDTH = 256
SLOTS = 96
OWNER_CAP = 4
CAP = SIDE * CORES * OWNER_CAP
CODE_ROWS = 16
COUNT_LANE = 64
UNROLL = 16
CHUNK = 8
PACKED = CAP * TILE + CODE_ROWS
COLUMNS = CORES * SIDE * BLOCKS
TURNED = BLOCKS * WIDTH
PART = NODES // SIDE
SHIPPED = TURNED + PART * WIDTH // TILE
BF16 = jnp.bfloat16
F32 = jnp.float32
VMEM_LIMIT = 16 * 1024 * 1024
VMEM_MOST = 62 * 1024 * 1024

WHOLE = pl.BlockSpec(memory_space=pltpu.VMEM)
FAR = pl.BlockSpec(memory_space=pltpu.HBM)
ANY = pl.BlockSpec(memory_space=pl.ANY)
SCALARS = pl.BlockSpec(memory_space=pltpu.SMEM)


def params(limit=VMEM_LIMIT):
    return pltpu.CompilerParams(vmem_limit_bytes=limit)


def struct(shape, dtype):
    return jax.ShapeDtypeStruct(shape, dtype)


def cost(flops, nbytes):
    return pl.CostEstimate(flops=int(flops), bytes_accessed=int(nbytes), transcendentals=0)


def move(array, axis, step):
    pairs = []
    for x in range(SIDE):
        for y in range(SIDE):
            for c in range(CORES):
                ahead = step * (1 - 2 * c)
                to_x = (x + ahead) % SIDE if axis == "x" else x
                to_y = (y + ahead) % SIDE if axis == "y" else y
                to_c = (c + step) % CORES if axis == "c" else c
                pairs.append(((x * SIDE + y) * CORES + c, (to_x * SIDE + to_y) * CORES + to_c))
    return lax.ppermute(array, "col", pairs)


def reshuffle(payload):
    devices = lax.axis_size("row") * lax.axis_size("col")
    direct = payload.reshape(devices, NODES // devices, WIDTH)
    moved = lax.all_to_all(direct, ("row", "col"), split_axis=0, concat_axis=0, tiled=True)
    return moved.reshape(payload.shape)


def exchange_planes(payload):
    rows, columns = lax.axis_size("row"), lax.axis_size("col")
    groups = [
        [z * columns + (x * SIDE + y) * CORES + c for z in range(rows) for x in range(SIDE) for c in range(CORES)]
        for y in range(SIDE)
    ]
    direct = payload.reshape(len(groups[0]), NODES // len(groups[0]), WIDTH)
    moved = lax.all_to_all(
        direct, ("row", "col"), split_axis=0, concat_axis=0, tiled=True, axis_index_groups=groups
    )
    return moved.reshape(payload.shape)


def ordering(key_row, key_col):
    below = (key_col[...] < key_row[...]).astype(jnp.int32)
    rank = jnp.sum(below, axis=0, keepdims=True)
    spot = lax.broadcasted_iota(jnp.int32, (NODES, NODES), 0)
    return (spot == rank).astype(F32).astype(BF16)


def order_kernel(key_row, key_col, data, out):
    select = ordering(key_row, key_col)
    out[...] = jnp.dot(select, data[...], preferred_element_type=F32).astype(BF16)


def order_turned_kernel(key_row, key_col, data, out):
    select = ordering(key_row, key_col)
    total = jnp.zeros((NODES, WIDTH), F32)
    for b in range(BLOCKS):
        part = select[:, b * TILE : (b + 1) * TILE]
        block = data[b * WIDTH : (b + 1) * WIDTH, :]
        total += lax.dot_general(part, block, (((1,), (1,)), ((), ())), preferred_element_type=F32)
    out[...] = total.astype(BF16)


def restoring(key_row, key_col):
    below = (key_row[...] < key_col[...]).astype(jnp.int32)
    rank = jnp.sum(below, axis=1, keepdims=True)
    spot = lax.broadcasted_iota(jnp.int32, (NODES, NODES), 1)
    return (spot == rank).astype(F32).astype(BF16)


def restore_kernel(key_row, key_col, data, out):
    select = restoring(key_row, key_col)
    out[...] = jnp.dot(select, data[...], preferred_element_type=F32).astype(BF16)


def select_kernel(key_row, key_col, out):
    out[...] = restoring(key_row, key_col)


def pick_kernel(select, data, out):
    out[...] = jnp.dot(select[...], data[...], preferred_element_type=F32).astype(BF16)


def selection(key):
    return pl.pallas_call(
        select_kernel,
        out_shape=struct((NODES, NODES), BF16),
        in_specs=[WHOLE] * 2,
        out_specs=WHOLE,
        compiler_params=params(),
        cost_estimate=cost(NODES * NODES * 8, 2 * NODES * NODES),
    )(key.reshape(1, NODES), key.reshape(NODES, 1))


def pick(select, data):
    return pl.pallas_call(
        pick_kernel,
        out_shape=struct((NODES, WIDTH), BF16),
        in_specs=[WHOLE] * 2,
        out_specs=WHOLE,
        compiler_params=params(),
        cost_estimate=cost(2 * NODES * NODES * WIDTH, 4 * NODES * WIDTH),
    )(select, data)


def ship_kernel(key_row, key_col, data, turned, *outs):
    select = ordering(key_row, key_col)
    ordered = jnp.dot(select, data[...], preferred_element_type=F32).astype(BF16)
    for k in range(SIDE):
        outs[k][:TURNED, :] = turned[...]
        for h in range(WIDTH // TILE):
            rows = slice(TURNED + h * PART, TURNED + (h + 1) * PART)
            outs[k][rows, :] = ordered[k * PART : (k + 1) * PART, h * TILE : (h + 1) * TILE]


def ship(key, data, turned):
    return pl.pallas_call(
        ship_kernel,
        out_shape=[struct((SHIPPED, TILE), BF16)] * SIDE,
        in_specs=[WHOLE] * 4,
        out_specs=[WHOLE] * SIDE,
        compiler_params=params(),
        cost_estimate=cost(2 * NODES * NODES * WIDTH, 8 * NODES * WIDTH),
    )(key.reshape(1, NODES), key.reshape(NODES, 1), data, turned)


def regroup_kernel(pair, *refs):
    shipped, out = refs[:SIDE], refs[SIDE]
    place = lax.broadcasted_iota(jnp.int32, (NODES, NODES), 0)
    held = lax.broadcasted_iota(jnp.int32, (NODES, NODES), 1)
    peer, step, row = (held % PART) // pair, held // PART, held % pair
    select = (place == (peer * SIDE + step) * pair + row).astype(F32).astype(BF16)
    for h in range(WIDTH // TILE):
        rows = slice(TURNED + h * PART, TURNED + (h + 1) * PART)
        data = jnp.concatenate([part[rows, :] for part in shipped], axis=0)
        total = jnp.dot(select, data, preferred_element_type=F32)
        out[:, h * TILE : (h + 1) * TILE] = total.astype(BF16)


def regroup(shipped, devices):
    return pl.pallas_call(
        functools.partial(regroup_kernel, NODES // devices),
        out_shape=struct((NODES, WIDTH), BF16),
        in_specs=[WHOLE] * SIDE,
        out_specs=WHOLE,
        compiler_params=params(),
        cost_estimate=cost(2 * NODES * NODES * WIDTH, 4 * NODES * WIDTH),
    )(*shipped)


def permute_call(kernel, key, data):
    return pl.pallas_call(
        kernel,
        out_shape=struct((NODES, WIDTH), BF16),
        in_specs=[WHOLE] * 3,
        out_specs=WHOLE,
        compiler_params=params(),
        cost_estimate=cost(2 * NODES * NODES * WIDTH, 4 * NODES * WIDTH),
    )(key.reshape(1, NODES), key.reshape(NODES, 1), data)


def bucket_kernel(target, code, source, *refs):
    outs, (tiles, packed, listed, counts, sent) = refs[:SIDE], refs[SIDE:]
    fetched = pltpu.make_async_copy(source, tiles, sent.at[SIDE])
    fetched.start()
    for d in range(SIDE + 1):
        counts[d] = 0

    def note(s, carry):
        d = target[s]
        n = counts[d]
        listed[d * SLOTS + n] = s
        counts[d] = n + 1
        return carry

    lax.fori_loop(0, SLOTS, note, 0)
    fetched.wait()
    lane = lax.broadcasted_iota(jnp.int32, (CODE_ROWS, TILE), 1)
    copies = []
    for d in (1, 3, 2, 0):
        used = counts[d]

        def place(n, codes, d=d):
            s = listed[d * SLOTS + n]
            packed[d, pl.ds(pl.multiple_of(n * TILE, TILE), TILE), :] = tiles[s]
            return jnp.where(lane == n, code[s], codes)

        def clear(n, carry, d=d):
            rows = pl.ds(pl.multiple_of(n * TILE, TILE), TILE)
            packed[d, rows, :] = jnp.zeros((TILE, TILE), BF16)
            return carry

        codes = lax.fori_loop(0, used, place, jnp.zeros((CODE_ROWS, TILE), jnp.int32))
        lax.fori_loop(used, CAP, clear, 0)
        codes = jnp.where(lane == COUNT_LANE, used, codes)
        packed[d, CAP * TILE :, :] = codes.astype(F32).astype(BF16)
        copies.append(pltpu.make_async_copy(packed.at[d], outs[d], sent.at[d]))
        copies[-1].start()
    for copy in copies:
        copy.wait()


def bucket(tiles, target, code):
    return pl.pallas_call(
        bucket_kernel,
        out_shape=[struct((PACKED, TILE), BF16)] * SIDE,
        in_specs=[SCALARS, SCALARS, FAR],
        out_specs=[FAR] * SIDE,
        scratch_shapes=[
            pltpu.VMEM((SLOTS, TILE, TILE), BF16),
            pltpu.VMEM((SIDE, PACKED, TILE), BF16),
            pltpu.SMEM(((SIDE + 1) * SLOTS,), jnp.int32),
            pltpu.SMEM((SIDE + 1,), jnp.int32),
            pltpu.SemaphoreType.DMA((SIDE + 1,)),
        ],
        compiler_params=params(VMEM_MOST),
        cost_estimate=cost(1e6, 7e6),
    )(target, code, tiles)


def fetch_packs(codes, packs, tiles, arrived):
    rows = CHUNK * TILE
    waits = []
    for k in range(SIDE):
        for i in range(CAP // CHUNK):
            source = packs[k].at[pl.ds(i * rows, rows)]
            place = tiles.at[pl.ds(k * CAP * TILE + i * rows, rows)]
            copy = pltpu.make_async_copy(source, place, arrived.at[k * (CAP // CHUNK) + i])
            used = codes[k * TILE + COUNT_LANE] > i * CHUNK
            pl.when(used)(copy.start)
            waits.append((used, copy))

    def wait():
        for used, copy in waits:
            pl.when(used)(copy.wait)

    return wait


def list_slots(codes, slots):
    total = jnp.int32(0)
    for k in range(SIDE):

        def note(n, at, k=k):
            code = codes[k * TILE + n]
            slots[0, at] = k * CAP + n
            slots[1, at] = k * BLOCKS + code // COLUMNS
            slots[2, at] = code % COLUMNS
            return at + 1

        total = lax.fori_loop(0, codes[k * TILE + COUNT_LANE], note, total)
    for u in range(UNROLL):
        slots[0, total + u] = SIDE * CAP
        slots[1, total + u] = 0
        slots[2, total + u] = 0
    return (total + UNROLL - 1) // UNROLL


def slot_block(slots, i, at, size):
    return pl.ds(pl.multiple_of(slots[i, at] * size, size), size)


def fetch(sources, places, arrived):
    copies = [
        pltpu.make_async_copy(source, place, arrived.at[i])
        for i, (source, place) in enumerate(zip(sources, places, strict=True))
    ]
    for copy in copies:
        copy.start()
    return copies


def forward_kernel(codes, *refs):
    packs, refs = refs[:SIDE], refs[SIDE:]
    shards, refs = refs[: CORES * SIDE], refs[CORES * SIDE :]
    outs, (tiles, features, totals, slots, arrived, fetched) = refs[:SIDE], refs[SIDE:]
    places = [features.at[pl.ds(j * NODES, NODES)] for j in range(CORES * SIDE)]
    wait = fetch_packs(codes, packs, tiles, fetched)
    copies = fetch(shards, places, arrived)
    totals[...] = jnp.zeros(totals.shape, F32)
    tiles[SIDE * CAP * TILE :, :] = jnp.zeros((TILE, TILE), BF16)
    steps = list_slots(codes, slots)
    for copy in copies:
        copy.wait()
    wait()

    def step(i, carry):
        for u in range(UNROLL):
            at = i * UNROLL + u
            tile = tiles[slot_block(slots, 0, at, TILE), :]
            block = features[slot_block(slots, 2, at, TILE), :]
            to = slot_block(slots, 1, at, TILE)
            totals[to, :] += jnp.dot(tile, block, preferred_element_type=F32)
        return carry

    lax.fori_loop(0, steps, step, 0)
    for k in range(SIDE):
        outs[k][...] = totals[k * NODES : (k + 1) * NODES, :].astype(outs[k].dtype)


def forward_product(packs, codes, shards):
    shape = (NODES, WIDTH)
    inputs = SIDE + CORES * SIDE
    return pl.pallas_call(
        forward_kernel,
        out_shape=[struct(shape, dtype) for dtype in (F32, BF16, BF16, F32)],
        in_specs=[SCALARS] + [ANY] * inputs,
        out_specs=[WHOLE] * SIDE,
        scratch_shapes=[
            pltpu.VMEM(((SIDE * CAP + 1) * TILE, TILE), BF16),
            pltpu.VMEM((CORES * SIDE * NODES, WIDTH), BF16),
            pltpu.VMEM((SIDE * NODES, WIDTH), F32),
            pltpu.SMEM((3, SIDE * CAP + UNROLL), jnp.int32),
            pltpu.SemaphoreType.DMA((CORES * SIDE,)),
            pltpu.SemaphoreType.DMA((SIDE * CAP // CHUNK,)),
        ],
        compiler_params=params(),
        cost_estimate=cost(6e9, 1e6),
    )(codes, *packs, *shards)


def backward_kernel(codes, *refs):
    packs, refs = refs[:SIDE], refs[SIDE:]
    shards, refs = refs[:SIDE], refs[SIDE:]
    near, refs = refs[:SIDE], refs[SIDE:]
    far, tiles, turned, totals, slots, arrived, fetched = refs
    places = [turned.at[pl.ds(k * TURNED, TURNED)] for k in range(SIDE)]
    wait = fetch_packs(codes, packs, tiles, fetched)
    copies = fetch([shard.at[pl.ds(0, TURNED)] for shard in shards], places, arrived)
    totals[...] = jnp.zeros(totals.shape, F32)
    tiles[SIDE * CAP * TILE :, :] = jnp.zeros((TILE, TILE), BF16)
    steps = list_slots(codes, slots)
    for copy in copies:
        copy.wait()
    wait()

    def step(i, carry):
        for u in range(UNROLL):
            at = i * UNROLL + u
            tile = tiles[slot_block(slots, 0, at, TILE), :]
            block = turned[slot_block(slots, 1, at, WIDTH), :]
            to = slot_block(slots, 2, at, WIDTH)
            totals[to, :] += jnp.dot(block, tile, preferred_element_type=F32)
        return carry

    lax.fori_loop(0, steps, step, 0)
    for j in range(SIDE):
        near[j][...] = totals[j * TURNED : (j + 1) * TURNED, :].astype(near[j].dtype)
    far[...] = totals[SIDE * TURNED :, :].astype(BF16)


def backward_product(packs, codes, shards):
    *near, far = pl.pallas_call(
        backward_kernel,
        out_shape=[struct((TURNED, TILE), F32)]
        + [struct((TURNED, TILE), BF16)] * (SIDE - 1)
        + [struct((SIDE * TURNED, TILE), BF16)],
        in_specs=[SCALARS] + [ANY] * (2 * SIDE),
        out_specs=[WHOLE] * (SIDE + 1),
        scratch_shapes=[
            pltpu.VMEM(((SIDE * CAP + 1) * TILE, TILE), BF16),
            pltpu.VMEM((SIDE * TURNED, TILE), BF16),
            pltpu.VMEM((CORES * SIDE * TURNED, TILE), F32),
            pltpu.SMEM((3, SIDE * CAP + UNROLL), jnp.int32),
            pltpu.SemaphoreType.DMA((SIDE,)),
            pltpu.SemaphoreType.DMA((SIDE * CAP // CHUNK,)),
        ],
        compiler_params=params(),
        cost_estimate=cost(6e9, 1e6),
    )(codes, *packs, *shards)
    return near, far


ORDER = (2, 1, 3)


def gather_line(array, axis):
    got = {d: move(array, axis, d) for d in ORDER}
    return [array] + [got[d] for d in range(1, SIDE)]


def gather_forward(features):
    one, three = move(features, "x", 1), move(features, "x", -1)
    line = [features, one, move(one, "x", 1), three]
    return line, line + [move(shard, "c", 1) for shard in line]


def scatter_forward(rows):
    passed, back = move(rows[2], "y", 1), move(rows[1], "y", -1)
    ahead = move((rows[3] + passed.astype(F32)).astype(BF16), "y", 1)
    return rows[0] + back.astype(F32) + ahead.astype(F32), back


def add_cores(near, far):
    parts = [slice(j * TURNED, (j + 1) * TURNED) for j in range(SIDE)]
    pairs = zip(near, parts, strict=True)
    return [own.astype(F32) + far[part].astype(F32) for own, part in pairs]


def add_up(own, arrived):
    for term in arrived:
        own = own + term.astype(F32)
    return own


def after(arrays, others):
    return lax.optimization_barrier((arrays, others))[0]


def shards(
    embeddings,
    partition_source,
    hash_target,
    tile_values,
    tile_row,
    tile_owner,
    tile_sub,
    tile_count,
    cotangent,
):
    index = lax.axis_index("col")
    core = index % CORES
    own_y = (index // CORES) % SIDE
    own_x = index // (CORES * SIDE)

    owner = tile_owner[:, 0]
    live = jnp.arange(SLOTS, dtype=jnp.int32) < tile_count[0]
    back_x = ((own_x - owner // (CORES * SIDE)) * (1 - 2 * (owner % CORES))) % SIDE
    far_y = ((owner // CORES - own_y) * (1 - 2 * core)) % SIDE
    side = (owner + core) % CORES
    column = (side * SIDE + back_x) * BLOCKS + tile_sub
    target = jnp.where(live, far_y, SIDE)
    devices = lax.axis_size("row") * lax.axis_size("col")
    turn = 1 - 2 * core

    def by_plane(device):
        return device // (CORES * SIDE) * CORES + device % CORES, device // CORES % SIDE

    plane, line_y = by_plane(hash_target // NODES)
    key = ((line_y - own_y) * turn) % SIDE * (devices // SIDE) + plane
    turned = cotangent.reshape(BLOCKS, TILE, WIDTH).transpose(0, 2, 1).reshape(TURNED, TILE)
    shipped = ship(key * NODES + hash_target % NODES, embeddings, turned)
    packs = bucket(tile_values, after(target, shipped[0]), tile_row * COLUMNS + column)
    shipped = [shipped[0]] + [move(shipped[k], "y", k) for k in range(1, SIDE)]
    moved = {d: move(after(packs[d], shipped[1]), "y", d) for d in ORDER}

    incoming = exchange_planes(regroup(shipped, devices))
    plane, line_y = by_plane(partition_source // NODES)
    turn = 1 - 2 * (plane % CORES)
    key = plane * SIDE + ((own_y - line_y) * turn) % SIDE
    place = jnp.arange(NODES, dtype=jnp.int32)
    initial = permute_call(restore_kernel, key * NODES + place, incoming)
    part_key = (partition_source // NODES) * NODES + place
    packs = [packs[0]] + [moved[d] for d in range(1, SIDE)]
    codes = jnp.concatenate([pack[CAP * TILE] for pack in packs]).astype(jnp.int32)
    line, features = gather_forward(initial)

    def both_products(features, gradients, beside):
        near, far = backward_product(packs, codes, gradients)
        far = move(far, "c", 1)
        if beside:
            rows = forward_product(packs, codes, after(features, near))
            near = after(near, rows[0])
        columns = add_cores(near, far)
        got = {j: move(columns[j].astype(BF16), "x", -j) for j in ORDER}
        if beside:
            rows = after(rows, columns)
        else:
            rows = forward_product(packs, codes, after(features, columns))
            columns[0] = after(columns[0], rows[0])
        total, arrived = scatter_forward(rows)
        if beside:
            columns[0] = after(columns[0], arrived)
        return total, add_up(columns[0], got.values())

    packs = after(packs, line)
    layer_one, back_one = both_products(features, shipped, True)
    layer_one = layer_one.astype(BF16)
    middle = ((turned.astype(F32) + back_one) / 3.0).astype(BF16)
    gradients = gather_line(middle, "y")
    line, features = gather_forward(after(layer_one, middle))
    layer_two, back_zero = both_products(features, after(gradients, line), False)
    grad_part = (turned.astype(F32) / 3.0 + back_zero).astype(BF16)
    returned = reshuffle(permute_call(order_turned_kernel, part_key, grad_part))
    embed_grad = pick(selection(hash_target), returned)
    propagated = ((initial.astype(F32) + layer_one.astype(F32) + layer_two) / 3.0).astype(BF16)
    return propagated, embed_grad


def solution(mesh):
    both = ("row", "col")
    return jax.shard_map(
        shards,
        mesh=mesh,
        in_specs=(
            P(both, None),
            P(both),
            P(both),
            P(both, None, None),
            P(both),
            P(both, None),
            P(both),
            P(both),
            P(both, None),
        ),
        out_specs=(P(both, None), P(both, None)),
        check_vma=False,
    )
```

```python
import functools

import jax
import jax.numpy as jnp
from jax import lax
from jax.experimental import pallas as pl
from jax.experimental.pallas import tpu as pltpu
from jax.sharding import PartitionSpec as P

SIDE = 4
CORES = 2
TILE = 128
NODES = 512
BLOCKS = NODES // TILE
WIDTH = 256
SLOTS = 96
OWNER_CAP = 4
CAP = SIDE * CORES * OWNER_CAP
CODE_ROWS = 16
COUNT_LANE = 64
UNROLL = 32
CHUNK = 8
PACKED = CAP * TILE + CODE_ROWS
COLUMNS = CORES * SIDE * BLOCKS
TURNED = BLOCKS * WIDTH
PART = NODES // SIDE
SHIPPED = TURNED + PART * WIDTH // TILE
BF16 = jnp.bfloat16
F32 = jnp.float32
VMEM_LIMIT = 16 * 1024 * 1024
VMEM_MOST = 62 * 1024 * 1024

WHOLE = pl.BlockSpec(memory_space=pltpu.VMEM)
FAR = pl.BlockSpec(memory_space=pltpu.HBM)
ANY = pl.BlockSpec(memory_space=pl.ANY)
SCALARS = pl.BlockSpec(memory_space=pltpu.SMEM)


def params(limit=VMEM_LIMIT):
    return pltpu.CompilerParams(vmem_limit_bytes=limit)


def struct(shape, dtype):
    return jax.ShapeDtypeStruct(shape, dtype)


def cost(flops, nbytes):
    return pl.CostEstimate(flops=int(flops), bytes_accessed=int(nbytes), transcendentals=0)


def move(array, axis, step):
    pairs = []
    for x in range(SIDE):
        for y in range(SIDE):
            for c in range(CORES):
                ahead = step * (1 - 2 * c)
                to_x = (x + ahead) % SIDE if axis == "x" else x
                to_y = (y + ahead) % SIDE if axis == "y" else y
                to_c = (c + step) % CORES if axis == "c" else c
                pairs.append(((x * SIDE + y) * CORES + c, (to_x * SIDE + to_y) * CORES + to_c))
    return lax.ppermute(array, "col", pairs)


def reshuffle(payload):
    devices = lax.axis_size("row") * lax.axis_size("col")
    direct = payload.reshape(devices, NODES // devices, WIDTH)
    moved = lax.all_to_all(direct, ("row", "col"), split_axis=0, concat_axis=0, tiled=True)
    return moved.reshape(payload.shape)


def exchange_planes(payload):
    rows, columns = lax.axis_size("row"), lax.axis_size("col")
    groups = [
        [z * columns + (x * SIDE + y) * CORES + c for z in range(rows) for x in range(SIDE) for c in range(CORES)]
        for y in range(SIDE)
    ]
    direct = payload.reshape(len(groups[0]), NODES // len(groups[0]), WIDTH)
    moved = lax.all_to_all(
        direct, ("row", "col"), split_axis=0, concat_axis=0, tiled=True, axis_index_groups=groups
    )
    return moved.reshape(payload.shape)


def ordering(key_row, key_col):
    below = (key_col[...] < key_row[...]).astype(jnp.int32)
    rank = jnp.sum(below, axis=0, keepdims=True)
    spot = lax.broadcasted_iota(jnp.int32, (NODES, NODES), 0)
    return (spot == rank).astype(F32).astype(BF16)


def order_kernel(key_row, key_col, data, out):
    select = ordering(key_row, key_col)
    out[...] = jnp.dot(select, data[...], preferred_element_type=F32).astype(BF16)


def order_turned_kernel(key_row, key_col, data, out):
    select = ordering(key_row, key_col)
    total = jnp.zeros((NODES, WIDTH), F32)
    for b in range(BLOCKS):
        part = select[:, b * TILE : (b + 1) * TILE]
        block = data[b * WIDTH : (b + 1) * WIDTH, :]
        total += lax.dot_general(part, block, (((1,), (1,)), ((), ())), preferred_element_type=F32)
    out[...] = total.astype(BF16)


def restore_kernel(key_row, key_col, data, out):
    below = (key_row[...] < key_col[...]).astype(jnp.int32)
    rank = jnp.sum(below, axis=1, keepdims=True)
    spot = lax.broadcasted_iota(jnp.int32, (NODES, NODES), 1)
    select = (spot == rank).astype(F32).astype(BF16)
    out[...] = jnp.dot(select, data[...], preferred_element_type=F32).astype(BF16)


def ship_kernel(key_row, key_col, data, turned, *outs):
    select = ordering(key_row, key_col)
    ordered = jnp.dot(select, data[...], preferred_element_type=F32).astype(BF16)
    for k in range(SIDE):
        outs[k][:TURNED, :] = turned[...]
        for h in range(WIDTH // TILE):
            rows = slice(TURNED + h * PART, TURNED + (h + 1) * PART)
            outs[k][rows, :] = ordered[k * PART : (k + 1) * PART, h * TILE : (h + 1) * TILE]


def ship(key, data, turned):
    return pl.pallas_call(
        ship_kernel,
        out_shape=[struct((SHIPPED, TILE), BF16)] * SIDE,
        in_specs=[WHOLE] * 4,
        out_specs=[WHOLE] * SIDE,
        compiler_params=params(),
        cost_estimate=cost(2 * NODES * NODES * WIDTH, 8 * NODES * WIDTH),
    )(key.reshape(1, NODES), key.reshape(NODES, 1), data, turned)


def regroup_kernel(pair, *refs):
    shipped, out = refs[:SIDE], refs[SIDE]
    place = lax.broadcasted_iota(jnp.int32, (NODES, NODES), 0)
    held = lax.broadcasted_iota(jnp.int32, (NODES, NODES), 1)
    peer, step, row = (held % PART) // pair, held // PART, held % pair
    select = (place == (peer * SIDE + step) * pair + row).astype(F32).astype(BF16)
    for h in range(WIDTH // TILE):
        rows = slice(TURNED + h * PART, TURNED + (h + 1) * PART)
        data = jnp.concatenate([part[rows, :] for part in shipped], axis=0)
        total = jnp.dot(select, data, preferred_element_type=F32)
        out[:, h * TILE : (h + 1) * TILE] = total.astype(BF16)


def regroup(shipped, devices):
    return pl.pallas_call(
        functools.partial(regroup_kernel, NODES // devices),
        out_shape=struct((NODES, WIDTH), BF16),
        in_specs=[WHOLE] * SIDE,
        out_specs=WHOLE,
        compiler_params=params(),
        cost_estimate=cost(2 * NODES * NODES * WIDTH, 4 * NODES * WIDTH),
    )(*shipped)


def permute_call(kernel, key, data):
    return pl.pallas_call(
        kernel,
        out_shape=struct((NODES, WIDTH), BF16),
        in_specs=[WHOLE] * 3,
        out_specs=WHOLE,
        compiler_params=params(),
        cost_estimate=cost(2 * NODES * NODES * WIDTH, 4 * NODES * WIDTH),
    )(key.reshape(1, NODES), key.reshape(NODES, 1), data)


def bucket_kernel(target, code, source, *refs):
    outs, (tiles, packed, listed, counts, sent) = refs[:SIDE], refs[SIDE:]
    fetched = pltpu.make_async_copy(source, tiles, sent.at[SIDE])
    fetched.start()
    for d in range(SIDE + 1):
        counts[d] = 0

    def note(s, carry):
        d = target[s]
        n = counts[d]
        listed[d * SLOTS + n] = s
        counts[d] = n + 1
        return carry

    lax.fori_loop(0, SLOTS, note, 0)
    fetched.wait()
    lane = lax.broadcasted_iota(jnp.int32, (CODE_ROWS, TILE), 1)
    copies = []
    for d in (1, 3, 2, 0):
        used = counts[d]

        def place(n, codes, d=d):
            s = listed[d * SLOTS + n]
            packed[d, pl.ds(pl.multiple_of(n * TILE, TILE), TILE), :] = tiles[s]
            return jnp.where(lane == n, code[s], codes)

        def clear(n, carry, d=d):
            rows = pl.ds(pl.multiple_of(n * TILE, TILE), TILE)
            packed[d, rows, :] = jnp.zeros((TILE, TILE), BF16)
            return carry

        codes = lax.fori_loop(0, used, place, jnp.zeros((CODE_ROWS, TILE), jnp.int32))
        lax.fori_loop(used, CAP, clear, 0)
        codes = jnp.where(lane == COUNT_LANE, used, codes)
        packed[d, CAP * TILE :, :] = codes.astype(F32).astype(BF16)
        copies.append(pltpu.make_async_copy(packed.at[d], outs[d], sent.at[d]))
        copies[-1].start()
    for copy in copies:
        copy.wait()


def bucket(tiles, target, code):
    return pl.pallas_call(
        bucket_kernel,
        out_shape=[struct((PACKED, TILE), BF16)] * SIDE,
        in_specs=[SCALARS, SCALARS, FAR],
        out_specs=[FAR] * SIDE,
        scratch_shapes=[
            pltpu.VMEM((SLOTS, TILE, TILE), BF16),
            pltpu.VMEM((SIDE, PACKED, TILE), BF16),
            pltpu.SMEM(((SIDE + 1) * SLOTS,), jnp.int32),
            pltpu.SMEM((SIDE + 1,), jnp.int32),
            pltpu.SemaphoreType.DMA((SIDE + 1,)),
        ],
        compiler_params=params(VMEM_MOST),
        cost_estimate=cost(1e6, 7e6),
    )(target, code, tiles)


def fetch_packs(codes, packs, tiles, arrived):
    rows = CHUNK * TILE
    waits = []
    for k in range(SIDE):
        for i in range(CAP // CHUNK):
            source = packs[k].at[pl.ds(i * rows, rows)]
            place = tiles.at[pl.ds(k * CAP * TILE + i * rows, rows)]
            copy = pltpu.make_async_copy(source, place, arrived.at[k * (CAP // CHUNK) + i])
            used = codes[k * TILE + COUNT_LANE] > i * CHUNK
            pl.when(used)(copy.start)
            waits.append((used, copy))

    def wait():
        for used, copy in waits:
            pl.when(used)(copy.wait)

    return wait


def list_slots(codes, slots):
    total = jnp.int32(0)
    for k in range(SIDE):

        def note(n, at, k=k):
            code = codes[k * TILE + n]
            slots[0, at] = k * CAP + n
            slots[1, at] = k * BLOCKS + code // COLUMNS
            slots[2, at] = code % COLUMNS
            return at + 1

        total = lax.fori_loop(0, codes[k * TILE + COUNT_LANE], note, total)
    for u in range(UNROLL):
        slots[0, total + u] = SIDE * CAP
        slots[1, total + u] = 0
        slots[2, total + u] = 0
    return (total + UNROLL - 1) // UNROLL


def slot_block(slots, i, at, size):
    return pl.ds(pl.multiple_of(slots[i, at] * size, size), size)


def fetch(sources, places, arrived):
    copies = [
        pltpu.make_async_copy(source, place, arrived.at[i])
        for i, (source, place) in enumerate(zip(sources, places, strict=True))
    ]
    for copy in copies:
        copy.start()
    return copies


def forward_kernel(codes, *refs):
    packs, refs = refs[:SIDE], refs[SIDE:]
    shards, refs = refs[: CORES * SIDE], refs[CORES * SIDE :]
    outs, (tiles, features, totals, slots, arrived, fetched) = refs[:SIDE], refs[SIDE:]
    places = [features.at[pl.ds(j * NODES, NODES)] for j in range(CORES * SIDE)]
    wait = fetch_packs(codes, packs, tiles, fetched)
    copies = fetch(shards, places, arrived)
    totals[...] = jnp.zeros(totals.shape, F32)
    tiles[SIDE * CAP * TILE :, :] = jnp.zeros((TILE, TILE), BF16)
    steps = list_slots(codes, slots)
    for copy in copies:
        copy.wait()
    wait()

    def step(i, carry):
        for u in range(UNROLL):
            at = i * UNROLL + u
            tile = tiles[slot_block(slots, 0, at, TILE), :]
            block = features[slot_block(slots, 2, at, TILE), :]
            to = slot_block(slots, 1, at, TILE)
            totals[to, :] += jnp.dot(tile, block, preferred_element_type=F32)
        return carry

    lax.fori_loop(0, steps, step, 0)
    for k in range(SIDE):
        outs[k][...] = totals[k * NODES : (k + 1) * NODES, :].astype(outs[k].dtype)


def forward_product(packs, codes, shards):
    shape = (NODES, WIDTH)
    inputs = SIDE + CORES * SIDE
    return pl.pallas_call(
        forward_kernel,
        out_shape=[struct(shape, dtype) for dtype in (F32, BF16, BF16, F32)],
        in_specs=[SCALARS] + [ANY] * inputs,
        out_specs=[WHOLE] * SIDE,
        scratch_shapes=[
            pltpu.VMEM(((SIDE * CAP + 1) * TILE, TILE), BF16),
            pltpu.VMEM((CORES * SIDE * NODES, WIDTH), BF16),
            pltpu.VMEM((SIDE * NODES, WIDTH), F32),
            pltpu.SMEM((3, SIDE * CAP + UNROLL), jnp.int32),
            pltpu.SemaphoreType.DMA((CORES * SIDE,)),
            pltpu.SemaphoreType.DMA((SIDE * CAP // CHUNK,)),
        ],
        compiler_params=params(),
        cost_estimate=cost(6e9, 1e6),
    )(codes, *packs, *shards)


def backward_kernel(codes, *refs):
    packs, refs = refs[:SIDE], refs[SIDE:]
    shards, refs = refs[:SIDE], refs[SIDE:]
    near, refs = refs[:SIDE], refs[SIDE:]
    far, tiles, turned, totals, slots, arrived, fetched = refs
    places = [turned.at[pl.ds(k * TURNED, TURNED)] for k in range(SIDE)]
    wait = fetch_packs(codes, packs, tiles, fetched)
    copies = fetch([shard.at[pl.ds(0, TURNED)] for shard in shards], places, arrived)
    totals[...] = jnp.zeros(totals.shape, F32)
    tiles[SIDE * CAP * TILE :, :] = jnp.zeros((TILE, TILE), BF16)
    steps = list_slots(codes, slots)
    for copy in copies:
        copy.wait()
    wait()

    def step(i, carry):
        for u in range(UNROLL):
            at = i * UNROLL + u
            tile = tiles[slot_block(slots, 0, at, TILE), :]
            block = turned[slot_block(slots, 1, at, WIDTH), :]
            to = slot_block(slots, 2, at, WIDTH)
            totals[to, :] += jnp.dot(block, tile, preferred_element_type=F32)
        return carry

    lax.fori_loop(0, steps, step, 0)
    for j in range(SIDE):
        near[j][...] = totals[j * TURNED : (j + 1) * TURNED, :].astype(near[j].dtype)
    far[...] = totals[SIDE * TURNED :, :].astype(BF16)


def backward_product(packs, codes, shards):
    *near, far = pl.pallas_call(
        backward_kernel,
        out_shape=[struct((TURNED, TILE), F32)]
        + [struct((TURNED, TILE), BF16)] * (SIDE - 1)
        + [struct((SIDE * TURNED, TILE), BF16)],
        in_specs=[SCALARS] + [ANY] * (2 * SIDE),
        out_specs=[WHOLE] * (SIDE + 1),
        scratch_shapes=[
            pltpu.VMEM(((SIDE * CAP + 1) * TILE, TILE), BF16),
            pltpu.VMEM((SIDE * TURNED, TILE), BF16),
            pltpu.VMEM((CORES * SIDE * TURNED, TILE), F32),
            pltpu.SMEM((3, SIDE * CAP + UNROLL), jnp.int32),
            pltpu.SemaphoreType.DMA((SIDE,)),
            pltpu.SemaphoreType.DMA((SIDE * CAP // CHUNK,)),
        ],
        compiler_params=params(),
        cost_estimate=cost(6e9, 1e6),
    )(codes, *packs, *shards)
    return near, far


ORDER = (2, 1, 3)


def gather_line(array, axis):
    got = {d: move(array, axis, d) for d in ORDER}
    return [array] + [got[d] for d in range(1, SIDE)]


def gather_forward(features):
    one, three = move(features, "x", 1), move(features, "x", -1)
    line = [features, one, move(one, "x", 1), three]
    return line, line + [move(shard, "c", 1) for shard in line]


def scatter_forward(rows):
    passed, back = move(rows[2], "y", 1), move(rows[1], "y", -1)
    ahead = move((rows[3] + passed.astype(F32)).astype(BF16), "y", 1)
    return rows[0] + back.astype(F32) + ahead.astype(F32), back


def add_cores(near, far):
    parts = [slice(j * TURNED, (j + 1) * TURNED) for j in range(SIDE)]
    pairs = zip(near, parts, strict=True)
    return [own.astype(F32) + far[part].astype(F32) for own, part in pairs]


def add_up(own, arrived):
    for term in arrived:
        own = own + term.astype(F32)
    return own


def after(arrays, others):
    return lax.optimization_barrier((arrays, others))[0]


def shards(
    embeddings,
    partition_source,
    hash_target,
    tile_values,
    tile_row,
    tile_owner,
    tile_sub,
    tile_count,
    cotangent,
):
    index = lax.axis_index("col")
    core = index % CORES
    own_y = (index // CORES) % SIDE
    own_x = index // (CORES * SIDE)

    owner = tile_owner[:, 0]
    live = jnp.arange(SLOTS, dtype=jnp.int32) < tile_count[0]
    back_x = ((own_x - owner // (CORES * SIDE)) * (1 - 2 * (owner % CORES))) % SIDE
    far_y = ((owner // CORES - own_y) * (1 - 2 * core)) % SIDE
    side = (owner + core) % CORES
    column = (side * SIDE + back_x) * BLOCKS + tile_sub
    target = jnp.where(live, far_y, SIDE)
    devices = lax.axis_size("row") * lax.axis_size("col")
    turn = 1 - 2 * core

    def by_plane(device):
        return device // (CORES * SIDE) * CORES + device % CORES, device // CORES % SIDE

    plane, line_y = by_plane(hash_target // NODES)
    key = ((line_y - own_y) * turn) % SIDE * (devices // SIDE) + plane
    turned = cotangent.reshape(BLOCKS, TILE, WIDTH).transpose(0, 2, 1).reshape(TURNED, TILE)
    shipped = ship(key * NODES + hash_target % NODES, embeddings, turned)
    packs = bucket(tile_values, after(target, shipped[0]), tile_row * COLUMNS + column)
    shipped = [shipped[0]] + [move(shipped[k], "y", k) for k in range(1, SIDE)]
    moved = {d: move(after(packs[d], shipped[1]), "y", d) for d in (1, 3)}
    moved[2] = move(after(packs[2], shipped), "y", 2)

    incoming = exchange_planes(regroup(shipped, devices))
    plane, line_y = by_plane(partition_source // NODES)
    turn = 1 - 2 * (plane % CORES)
    key = plane * SIDE + ((own_y - line_y) * turn) % SIDE
    place = jnp.arange(NODES, dtype=jnp.int32)
    initial = permute_call(restore_kernel, key * NODES + place, incoming)
    part_key = (partition_source // NODES) * NODES + place
    packs = [packs[0]] + [moved[d] for d in range(1, SIDE)]
    codes = jnp.concatenate([pack[CAP * TILE] for pack in packs]).astype(jnp.int32)
    line, features = gather_forward(initial)

    def both_products(features, gradients, beside):
        near, far = backward_product(packs, codes, gradients)
        far = move(far, "c", 1)
        if beside:
            rows = forward_product(packs, codes, after(features, near))
            near = after(near, rows[0])
        columns = add_cores(near, far)
        got = {j: move(columns[j].astype(BF16), "x", -j) for j in ORDER}
        if beside:
            rows = after(rows, columns)
        else:
            rows = forward_product(packs, codes, after(features, columns))
            columns[0] = after(columns[0], rows[0])
        total, arrived = scatter_forward(rows)
        if beside:
            columns[0] = after(columns[0], arrived)
        return total, add_up(columns[0], got.values())

    packs = after(packs, line)
    layer_one, back_one = both_products(features, shipped, True)
    layer_one = layer_one.astype(BF16)
    middle = ((turned.astype(F32) + back_one) / 3.0).astype(BF16)
    gradients = gather_line(middle, "y")
    line, features = gather_forward(after(layer_one, middle))
    layer_two, back_zero = both_products(features, after(gradients, line), False)
    grad_part = (turned.astype(F32) / 3.0 + back_zero).astype(BF16)
    returned = reshuffle(permute_call(order_turned_kernel, part_key, grad_part))
    embed_grad = permute_call(restore_kernel, hash_target, returned)
    propagated = ((initial.astype(F32) + layer_one.astype(F32) + layer_two) / 3.0).astype(BF16)
    return propagated, embed_grad


def solution(mesh):
    both = ("row", "col")
    return jax.shard_map(
        shards,
        mesh=mesh,
        in_specs=(
            P(both, None),
            P(both),
            P(both),
            P(both, None, None),
            P(both),
            P(both, None),
            P(both),
            P(both),
            P(both, None),
        ),
        out_specs=(P(both, None), P(both, None)),
        check_vma=False,
    )
```
